256 devices in a mesh: region: 8 (over x, y_hi), slab: 32 (over z, y_lo, core).
Axes of the slice: x: 4, y: 4 (y_hi: 2, y_lo: 2; y = y_hi * 2 + y_lo), z: 8, core: 2. Of those that a mesh axis runs over, the one named last changes fastest.
Arguments:
- nodes: bfloat16 [32768, 256], P(('region', 'slab')), may hold values from -6 to 6
- edge_feats: bfloat16 [163840, 256], P(('region', 'slab')), may hold values from -6 to 6
- cotangent: float32 [32768, 256], P(('region', 'slab')), may hold values from -6 to 6
- edge_w1: bfloat16 [768, 256], replicated, may hold values from -0.21875 to 0.21875
- edge_w2: bfloat16 [256, 256], replicated, may hold values from -0.375 to 0.375
- node_w1: bfloat16 [512, 256], replicated, may hold values from -0.25 to 0.25
- node_w2: bfloat16 [256, 256], replicated, may hold values from -0.375 to 0.375
- ln_gain: float32 [256], replicated, may hold values from 0.1 to 1.9
- senders: int32 [163840], P(('region', 'slab')), may hold values from 0 to 255
- receivers: int32 [163840], P(('region', 'slab')), may hold values from 0 to 127
- send_rows: int32 [1024, 32], P(('region', 'slab')), may hold values from 0 to 127
- edge_count: int32 [8, 32], P('region', 'slab'), may hold values from 160 to 640, as said below
Outputs:
- node_grad: float32 [32768, 256], P(('region', 'slab'))
- edge_grad: float32 [163840, 256], P(('region', 'slab'))
- grad_edge_in: float32 [768, 256], replicated
- grad_edge_out: float32 [256, 256], replicated
- grad_node_in: float32 [512, 256], replicated
- grad_node_out: float32 [256, 256], replicated
- grad_gain: float32 [256], replicated
The draws below stay inside these ranges and needn't reach their ends.
Inputs may be any that keep to these rules, and one draw needn't show every extreme that they name: `senders`: index into the device's 128 own rows followed by its 128 halo rows. `receivers`: index into the device's own rows. `send_rows`: index into the device's own rows. `edge_count`: slots below it are live, the rest padding; some device has all 640 slots live.
All inputs are finite; a program needn't handle non-finite values.
Results may differ from the reference program's by a relative error of at most 0.019.
Values may be sent and summed in bfloat16 or wider, within the bound.
No kernel may reach another device: no remote copies, remote signals or barrier semaphores. Data moves between devices by JAX's collectives and lax.ppermute only.
A program may use at most 64 MiB of HBM per device.

```python
import jax
import jax.numpy as jnp
from jax import lax

L = 256
NODES_DEV = 128
EDGES_DEV = 640
HALO_ROWS = 32
STEPS = 4
NODES = 32768
EDGES = 163840
N_REGION = 8
N_SLAB = 32


def draw_edge_count(key, part):
    key = jax.random.fold_in(key, 7)
    first_key, second_key = jax.random.split(key)
    device_count = N_REGION * N_SLAB
    counts = jax.random.randint(first_key, (device_count,), EDGES_DEV // 4, 3 * EDGES_DEV // 5 + 1)
    fullest = jax.random.randint(second_key, (), 0, device_count)
    counts = jnp.where(jnp.arange(device_count) == fullest, EDGES_DEV, counts)
    return counts.reshape(N_REGION, N_SLAB).astype(jnp.int32)


def set_ends(drawn, stream_key, low, high):
    extent = drawn.shape
    place = [jax.random.randint(jax.random.fold_in(stream_key, axis), (), 0, extent[axis]) for axis in range(len(extent))]
    drawn = drawn.at[tuple(place)].set(low)
    longest = extent.index(max(extent))
    place[longest] = (place[longest] + 1) % extent[longest]
    return drawn.at[tuple(place)].set(high)


def block_levels(key, extent, pieces, least, top_value):
    factor_of, own = 1.0, jax.random.fold_in(key, 6)
    for dim, blocks in pieces:
        heights = jnp.exp(jax.random.uniform(jax.random.fold_in(own, dim), (blocks,), jnp.float32, least / len(pieces), top_value / len(pieces)))
        factor_of = factor_of * jnp.repeat(heights, extent[dim] // blocks).reshape([-1 if axis == dim else 1 for axis in range(len(extent))])
    return factor_of


def scatter_about(rng, shape, scale, limit, cuts=(), kind=jnp.bfloat16):
    array = jax.random.normal(rng, shape, jnp.float32) * scale
    if len(cuts) > 0:
        array = block_levels(rng, shape, cuts, -0.22, 0.18) * array
    return jnp.clip(array, min=-limit, max=limit).astype(kind)


def setup_inputs(seed: int = 0) -> dict:
    arg_keys = jax.random.split(jax.random.key(seed), 13)
    nodes = scatter_about(arg_keys[0], (NODES, L), 1.0, 6.0, ((0, 256),))
    edge_feats = scatter_about(arg_keys[1], (EDGES, L), 1.0, 6.0, ((0, 256),))
    cotangent = scatter_about(arg_keys[2], (NODES, L), 1.0, 6.0, ((0, 256),), jnp.float32)
    edge_w1 = scatter_about(arg_keys[3], (3 * L, L), (3 * L) ** -0.5, 0.21875)
    edge_w2 = scatter_about(arg_keys[4], (L, L), L ** -0.5, 0.375)
    node_w1 = scatter_about(arg_keys[5], (2 * L, L), (2 * L) ** -0.5, 0.25)
    node_w2 = scatter_about(arg_keys[6], (L, L), L ** -0.5, 0.375)
    ln_gain = jnp.clip(1.0 + 0.18 * jax.random.normal(arg_keys[7], (L,), jnp.float32), 0.1, 1.9)
    senders = set_ends(jax.random.randint(arg_keys[8], (EDGES,), 0, NODES_DEV + 4 * HALO_ROWS), jax.random.fold_in(arg_keys[8], 1), 0, (NODES_DEV + 4 * HALO_ROWS) - 1).astype(jnp.int32)
    receivers = set_ends(jax.random.randint(arg_keys[9], (EDGES,), 0, NODES_DEV), jax.random.fold_in(arg_keys[9], 1), 0, NODES_DEV - 1).astype(jnp.int32)
    send_rows = set_ends(jax.random.randint(arg_keys[10], (4 * N_REGION * N_SLAB, HALO_ROWS), 0, NODES_DEV), jax.random.fold_in(arg_keys[10], 1), 0, NODES_DEV - 1).astype(jnp.int32)
    edge_count = draw_edge_count(jax.random.fold_in(arg_keys[12], 71), 0)
    return {"nodes": nodes, "edge_feats": edge_feats, "cotangent": cotangent, "edge_w1": edge_w1, "edge_w2": edge_w2, "node_w1": node_w1, "node_w2": node_w2, "ln_gain": ln_gain, "senders": senders, "receivers": receivers, "send_rows": send_rows, "edge_count": edge_count}


EPS = 1e-05

def silu_slope(pre):
    sig = jax.nn.sigmoid(pre)
    return sig * (1.0 + pre * (1.0 - sig))

def edge_forward(extended, own_rows, edges, send_idx, recv_idx, live_mask, edge_w1, edge_w2):
    stacked = jnp.concatenate([extended[send_idx], own_rows[recv_idx], edges], axis=1)
    pre_edge = jnp.dot(stacked, edge_w1, preferred_element_type=jnp.float32)
    hidden_edge = jax.nn.silu(pre_edge).astype(jnp.bfloat16)
    message = jnp.dot(hidden_edge, edge_w2, preferred_element_type=jnp.float32) * live_mask[:, None]
    summed = jax.ops.segment_sum(message, recv_idx, num_segments=own_rows.shape[0])
    return (stacked, pre_edge, hidden_edge, summed)

def node_parts(own_rows, summed, node_w1, node_w2):
    joined = jnp.concatenate([own_rows, summed.astype(jnp.bfloat16)], axis=1)
    pre_node = jnp.dot(joined, node_w1, preferred_element_type=jnp.float32)
    hidden_node = jax.nn.silu(pre_node).astype(jnp.bfloat16)
    update = jnp.dot(hidden_node, node_w2, preferred_element_type=jnp.float32)
    centre = update - lax.optimization_barrier(jnp.mean(update, axis=-1, keepdims=True))
    inv_dev = lax.rsqrt(lax.optimization_barrier(jnp.mean(centre * centre, axis=-1, keepdims=True)) + EPS)
    return (joined, pre_node, hidden_node, centre * inv_dev, inv_dev)

def node_forward(own_rows, summed, node_w1, node_w2, ln_gain):
    normed = node_parts(own_rows, summed, node_w1, node_w2)[3]
    return (own_rows.astype(jnp.float32) + normed * ln_gain).astype(jnp.bfloat16)

def local_backward(extended, edges, send_idx, recv_idx, live_mask, upstream, weights):
    edge_w1, edge_w2, node_w1, node_w2, ln_gain = weights
    own_count = upstream.shape[0]
    width = upstream.shape[1]
    own_rows = extended[:own_count]
    stacked, pre_edge, hidden_edge, summed = edge_forward(extended, own_rows, edges, send_idx, recv_idx, live_mask, edge_w1, edge_w2)
    joined, pre_node, hidden_node, normed, inv_dev = node_parts(own_rows, summed, node_w1, node_w2)
    gain_term = lax.optimization_barrier(jnp.sum(upstream * normed, axis=0))
    scaled = upstream * ln_gain
    grad_update = inv_dev * (scaled - lax.optimization_barrier(jnp.mean(scaled, axis=-1, keepdims=True)) - normed * lax.optimization_barrier(jnp.mean(scaled * normed, axis=-1, keepdims=True)))
    grad_update = grad_update.astype(jnp.bfloat16)
    node_out_term = jnp.dot(hidden_node.T, grad_update, preferred_element_type=jnp.float32)
    grad_hidden = jnp.dot(grad_update, node_w2.T, preferred_element_type=jnp.float32)
    grad_pre_node = (grad_hidden * silu_slope(pre_node)).astype(jnp.bfloat16)
    node_in_term = jnp.dot(joined.T, grad_pre_node, preferred_element_type=jnp.float32)
    grad_joined = jnp.dot(grad_pre_node, node_w1.T, preferred_element_type=jnp.float32)
    grad_message = (grad_joined[:, width:][recv_idx] * live_mask[:, None]).astype(jnp.bfloat16)
    edge_out_term = jnp.dot(hidden_edge.T, grad_message, preferred_element_type=jnp.float32)
    grad_hidden_edge = jnp.dot(grad_message, edge_w2.T, preferred_element_type=jnp.float32)
    grad_pre_edge = (grad_hidden_edge * silu_slope(pre_edge)).astype(jnp.bfloat16)
    edge_in_term = jnp.dot(stacked.T, grad_pre_edge, preferred_element_type=jnp.float32)
    grad_stacked = jnp.dot(grad_pre_edge, edge_w1.T, preferred_element_type=jnp.float32)
    grad_extended = jax.ops.segment_sum(grad_stacked[:, :width], send_idx, num_segments=extended.shape[0])
    grad_own = upstream + grad_joined[:, :width] + grad_extended[:own_count]
    grad_own = grad_own + jax.ops.segment_sum(grad_stacked[:, width:2 * width], recv_idx, num_segments=own_count)
    terms = (edge_in_term, edge_out_term, node_in_term, node_out_term, gain_term)
    return (grad_own, grad_extended[own_count:], grad_stacked[:, 2 * width:], terms)

def incoming_rows(states, send_lists):
    width = states.shape[2]
    picked = jax.vmap(lambda state, lists: state[lists])(states, send_lists)
    picked = picked.reshape(N_REGION, N_SLAB, 4, HALO_ROWS, width)
    from_slab_before = jnp.roll(picked[:, :, 1], 1, axis=1)
    from_slab_after = jnp.roll(picked[:, :, 0], -1, axis=1)
    from_region_before = jnp.roll(picked[:, :, 3], 1, axis=0)
    from_region_after = jnp.roll(picked[:, :, 2], -1, axis=0)
    joined = jnp.stack([from_slab_before, from_slab_after, from_region_before, from_region_after], axis=2)
    return joined.reshape(N_REGION * N_SLAB, 4 * HALO_ROWS, width)

def returned_rows(grad_halo, send_lists):
    width = grad_halo.shape[2]
    blocks = grad_halo.reshape(N_REGION, N_SLAB, 4, HALO_ROWS, width)
    to_first = jnp.roll(blocks[:, :, 1], 1, axis=1)
    to_second = jnp.roll(blocks[:, :, 0], -1, axis=1)
    to_third = jnp.roll(blocks[:, :, 3], 1, axis=0)
    to_fourth = jnp.roll(blocks[:, :, 2], -1, axis=0)
    values = jnp.stack([to_first, to_second, to_third, to_fourth], axis=2).reshape(N_REGION * N_SLAB, 4 * HALO_ROWS, width)

    def land(lists, vals):
        return jnp.zeros((NODES_DEV, width), vals.dtype).at[lists.reshape(-1)].add(vals)
    return jax.vmap(land)(send_lists, values)

def reference(nodes, edge_feats, cotangent, edge_w1, edge_w2, node_w1, node_w2, ln_gain, senders, receivers, send_rows, edge_count):
    device_count = N_REGION * N_SLAB
    width = nodes.shape[1]
    states = nodes.reshape(device_count, NODES_DEV, width)
    edges = edge_feats.reshape(device_count, EDGES_DEV, width)
    send_idx = senders.reshape(device_count, EDGES_DEV)
    recv_idx = receivers.reshape(device_count, EDGES_DEV)
    send_lists = send_rows.reshape(device_count, 4, HALO_ROWS)
    live_masks = (jnp.arange(EDGES_DEV, dtype=jnp.int32)[None, :] < edge_count.reshape(device_count, 1)).astype(jnp.float32)
    weights = (edge_w1, edge_w2, node_w1, node_w2, ln_gain)
    extended_list = []
    for layer_index in range(STEPS):
        extended = jnp.concatenate([states, incoming_rows(states, send_lists)], axis=1)
        extended_list.append(extended)
        if layer_index + 1 < STEPS:

            def advance(packed):
                ext, edg, snd, rcv, live = packed
                own_rows = ext[:NODES_DEV]
                summed = edge_forward(ext, own_rows, edg, snd, rcv, live, edge_w1, edge_w2)[3]
                return node_forward(own_rows, summed, node_w1, node_w2, ln_gain)
            states = lax.map(advance, (extended, edges, send_idx, recv_idx, live_masks))
    upstream = cotangent.reshape(device_count, NODES_DEV, width)
    edge_total = jnp.zeros((device_count, EDGES_DEV, width), jnp.float32)
    totals = (jnp.zeros((3 * width, width), jnp.float32), jnp.zeros((width, width), jnp.float32), jnp.zeros((2 * width, width), jnp.float32), jnp.zeros((width, width), jnp.float32), jnp.zeros((width,), jnp.float32))
    for layer_index in reversed(range(STEPS)):

        def backward_one(carry, packed):
            ext, edg, snd, rcv, live, upper = packed
            grad_own, grad_halo, grad_edge, terms = local_backward(ext, edg, snd, rcv, live, upper, weights)
            return (tuple((c + t for c, t in zip(carry, terms))), (grad_own, grad_halo, grad_edge))
        totals, outcome = lax.scan(backward_one, totals, (extended_list[layer_index], edges, send_idx, recv_idx, live_masks, upstream))
        grad_own, grad_halo, grad_edge = outcome
        upstream = grad_own + returned_rows(grad_halo, send_lists)
        edge_total = edge_total + grad_edge
    factor = float(NODES) ** (-0.5)
    return (upstream.reshape(NODES, width), edge_total.reshape(EDGES, width), totals[0] * factor, totals[1] * factor, totals[2] * factor, totals[3] * factor, totals[4] * factor)
```

```python
import jax
import jax.numpy as jnp
from jax import lax
from jax.experimental import pallas as pl
from jax.experimental.pallas import tpu as pltpu
from jax.sharding import Mesh
from jax.sharding import PartitionSpec as P

STEPS = 4
EPS = 1e-05
L = 256
OWN = 128
HALO = 32
BF16 = jnp.bfloat16
F32 = jnp.float32
AXES = ("x", "yh", "z", "yl", "c")
REGION = ("x", "yh")
SLAB = ("z", "yl", "c")
PLANE = ("x", "yh", "yl")
CHUNKS = 16
CHUNK_ROWS = 64


def mm(a, b):
    return jnp.dot(a, b, preferred_element_type=F32)


def mm_t(a, b):
    return lax.dot_general(a, b, (((0,), (0,)), ((), ())), preferred_element_type=F32)


def split(v):
    high = v.astype(BF16)
    low = (v - high.astype(F32)).astype(BF16)
    return high, low


def mm_split(v, w):
    high, low = split(v)
    return mm(high, w) + mm(low, w)


def sigmoid(v):
    return 0.5 * jnp.tanh(0.5 * v) + 0.5


def call(kernel, outs, *args, smem=0, **kw):
    specs = [pl.BlockSpec(memory_space=pltpu.SMEM)] * smem
    specs += [pl.BlockSpec(memory_space=pltpu.VMEM)] * (len(args) - smem)
    return pl.pallas_call(
        kernel,
        out_shape=[jax.ShapeDtypeStruct(s, d) for s, d in outs],
        in_specs=specs,
        out_specs=[pl.BlockSpec(memory_space=pltpu.VMEM)] * len(outs),
        compiler_params=pltpu.CompilerParams(vmem_limit_bytes=32 * 1024 * 1024),
        **kw,
    )(*args)


def slot_lists(place, lists):
    slab_odd = place[1] % 2
    region_odd = place[0] % 2
    a, b, c, d = (lists[i : i + 1, :] for i in range(4))
    return (
        jnp.where(region_odd == 1, d, c),
        jnp.where(region_odd == 1, c, d),
        jnp.where(slab_odd == 1, b, a),
        jnp.where(slab_odd == 1, a, b),
    )


def first_kernel(place, nodes, lists, s0, s1, s2, s3, spread):
    h = nodes[...]
    row = lax.broadcasted_iota(jnp.int32, (OWN, HALO), 0)
    for i, (idx, out) in enumerate(zip(slot_lists(place, lists[...]), (s0, s1, s2, s3))):
        hot = (row == idx).astype(F32).astype(BF16)
        spread[:, i * HALO : (i + 1) * HALO] = hot
        out[...] = mm_t(hot, h).astype(BF16)


def prep_kernel(
    place, count, send_idx, recv_idx, feats, edge_w1, edge_w2, node_w1, node_w2,
    t_out, tt_out, s_out, st_out, fw_out, w1t_out, w2t_out, n1t_out, n2t_out,
):
    edges = feats.shape[0]
    lane = lax.broadcasted_iota(jnp.int32, (1, edges), 1)
    live = lane < count[0, 0]
    snd = send_idx[...]
    off = snd - OWN
    slab_swap = jnp.where(place[1] % 2 == 1, 3 * HALO, 2 * HALO)
    region_swap = jnp.where(place[0] % 2 == 1, 3 * HALO, 2 * HALO)
    flip = jnp.where(off < 2 * HALO, slab_swap, region_swap)
    snd = jnp.where(off >= 0, OWN + (off ^ flip), snd)
    snd = jnp.where(live, snd, -1)
    rcv = jnp.where(live, recv_idx[...], -1)
    tt = (lax.broadcasted_iota(jnp.int32, (2 * OWN, edges), 0) == snd).astype(F32)
    st = (lax.broadcasted_iota(jnp.int32, (OWN, edges), 0) == rcv).astype(F32)
    tt_out[...] = tt.astype(BF16)
    st_out[...] = st.astype(BF16)
    t_out[...] = tt.T.astype(BF16)
    s_out[...] = st.T.astype(BF16)
    w1 = edge_w1[...]
    fw_out[...] = mm(feats[...], w1[2 * L :])
    w1t_out[...] = w1.T
    w2t_out[...] = edge_w2[...].T
    n1t_out[...] = node_w1[...].T
    n2t_out[...] = node_w2[...].T


def forward_body(h, halo, t, s, st, fw, edge_w1, edge_w2, node_w1, node_w2):
    extended = jnp.concatenate([h] + halo, axis=0)
    from_send = mm(t, extended).astype(BF16)
    from_recv = mm(s, h).astype(BF16)
    pre = mm(from_send, edge_w1[:L]) + mm(from_recv, edge_w1[L : 2 * L]) + fw
    sig = sigmoid(pre)
    silu = pre * sig
    edge_slope = sig + silu * (1.0 - sig)
    hidden_sum = mm(st, silu.astype(BF16))
    summed = mm_split(hidden_sum, edge_w2).astype(BF16)
    pre_node = mm(h, node_w1[:L]) + mm(summed, node_w1[L:])
    sig_n = sigmoid(pre_node)
    silu_n = pre_node * sig_n
    node_slope = sig_n + silu_n * (1.0 - sig_n)
    hidden_node = silu_n.astype(BF16)
    update = mm(hidden_node, node_w2)
    centre = update - jnp.mean(update, axis=-1, keepdims=True)
    inv_dev = lax.rsqrt(jnp.mean(centre * centre, axis=-1, keepdims=True) + EPS)
    normed = centre * inv_dev
    return edge_slope, hidden_sum, summed, node_slope, hidden_node, normed, inv_dev


def forward_kernel(
    h_ref, p0, p1, p2, p3, t, s, st, fw, spread, edge_w1, edge_w2, node_w1, node_w2, gain,
    h_out, s0, s1, s2, s3, edge_slope_o, hidden_sum_o, summed_o, node_slope_o, hidden_node_o, normed_o, inv_dev_o,
):
    h = h_ref[...]
    parts = forward_body(
        h, [p0[...], p1[...], p2[...], p3[...]], t[...], s[...], st[...], fw[...],
        edge_w1, edge_w2[...], node_w1, node_w2[...],
    )
    edge_slope, hidden_sum, summed, node_slope, hidden_node, normed, inv_dev = parts
    nxt = (h.astype(F32) + normed * gain[...]).astype(BF16)
    h_out[...] = nxt
    sent = mm_t(spread[...], nxt).astype(BF16)
    for i, out in enumerate((s0, s1, s2, s3)):
        out[...] = sent[i * HALO : (i + 1) * HALO]
    edge_slope_o[...] = edge_slope
    hidden_sum_o[...] = hidden_sum
    summed_o[...] = summed
    node_slope_o[...] = node_slope
    hidden_node_o[...] = hidden_node
    normed_o[...] = normed
    inv_dev_o[...] = jnp.broadcast_to(inv_dev, inv_dev_o.shape)


def backward_body(
    up, parts, gain, s, st, tt, w1t, w2t, n1t, n2t,
    own_out, g0, g1, g2, g3, gpe_o, q_o, r_o, gpn_o, gu_o, gm_o, gain_o,
):
    edge_slope, node_slope, normed, inv_dev = parts
    gain_o[...] = jnp.sum(up * normed, axis=0, keepdims=True)
    scaled = up * gain
    gu = inv_dev * (
        scaled
        - jnp.mean(scaled, axis=-1, keepdims=True)
        - normed * jnp.mean(scaled * normed, axis=-1, keepdims=True)
    )
    gu = gu.astype(BF16)
    gpn = (mm(gu, n2t) * node_slope).astype(BF16)
    gj = mm(gpn, n1t)
    own_out[...] = up + gj[:, :L]
    gm = gj[:, L:].astype(BF16)
    high, low = split(mm(gm, w2t))
    s2 = jnp.concatenate([s, s], axis=1)
    ghe = mm(s2, jnp.concatenate([high, low], axis=0))
    gpe = (ghe * edge_slope).astype(BF16)
    q = mm(tt, gpe)
    r = mm(st, gpe)
    ge = mm_split(q, w1t[:, :L])
    own_out[...] = own_out[...] + ge[:OWN] + mm_split(r, w1t[:, L : 2 * L])
    for i, out in enumerate((g0, g1, g2, g3)):
        out[...] = ge[OWN + i * HALO : OWN + (i + 1) * HALO].astype(BF16)
    gpe_o[...] = gpe
    q_o[...] = q
    r_o[...] = r
    gpn_o[...] = gpn
    gu_o[...] = gu
    gm_o[...] = gm


def landed(own, spread, p0, p1, p2, p3):
    parts = jnp.concatenate([p0[...], p1[...], p2[...], p3[...]], axis=0)
    return own[...] + mm(spread[...], parts)


def turn_kernel(
    h_ref, p0, p1, p2, p3, t, s, st, fw, edge_w1, edge_w2, node_w1, node_w2, gain,
    cot, tt, w1t, w2t, n1t, n2t,
    own_out, g0, g1, g2, g3, gpe_o, q_o, r_o, gpn_o, gu_o, gm_o, gain_o, hidden_sum_o, summed_o, hidden_node_o,
):
    st_v, s_v = st[...], s[...]
    parts = forward_body(
        h_ref[...], [p0[...], p1[...], p2[...], p3[...]], t[...], s_v, st_v, fw[...],
        edge_w1, edge_w2[...], node_w1, node_w2[...],
    )
    edge_slope, hidden_sum, summed, node_slope, hidden_node, normed, inv_dev = parts
    hidden_sum_o[...] = hidden_sum
    summed_o[...] = summed
    hidden_node_o[...] = hidden_node
    backward_body(
        cot[...], (edge_slope, node_slope, normed, inv_dev), gain[...],
        s_v, st_v, tt[...], w1t, w2t[...], n1t[...], n2t[...],
        own_out, g0, g1, g2, g3, gpe_o, q_o, r_o, gpn_o, gu_o, gm_o, gain_o,
    )


def backward_kernel(
    own, p0, p1, p2, p3, spread, edge_slope, node_slope, normed, inv_dev, gain,
    s, st, tt, w1t, w2t, n1t, n2t,
    own_out, g0, g1, g2, g3, gpe_o, q_o, r_o, gpn_o, gu_o, gm_o, gain_o,
):
    up = landed(own, spread, p0, p1, p2, p3)
    backward_body(
        up, (edge_slope[...], node_slope[...], normed[...], inv_dev[:, :1]), gain[...],
        s[...], st[...], tt[...], w1t, w2t[...], n1t[...], n2t[...],
        own_out, g0, g1, g2, g3, gpe_o, q_o, r_o, gpn_o, gu_o, gm_o, gain_o,
    )


def weight_terms(h, halo, feats, hidden_sum, summed, hidden_node, gpe, q, r, gpn, gu, gm):
    extended = jnp.concatenate([h] + halo, axis=0)
    q_high, q_low = split(q)
    r_high, r_low = split(r)
    h_high, h_low = split(hidden_sum)
    return (
        mm_t(extended, q_high) + mm_t(extended, q_low),
        mm_t(h, r_high) + mm_t(h, r_low),
        mm_t(feats, gpe),
        mm_t(h_high, gm) + mm_t(h_low, gm),
        mm_t(h, gpn),
        mm_t(summed, gpn),
        mm_t(hidden_node, gu),
    )


def weight_args(refs):
    (h_ref, p0, p1, p2, p3, feats, hidden_sum, summed, hidden_node, gpe, q, r, gpn, gu, gm) = refs
    return weight_terms(
        h_ref[...], [p0[...], p1[...], p2[...], p3[...]], feats[...], hidden_sum[...], summed[...],
        hidden_node[...], gpe[...], q[...], r[...], gpn[...], gu[...], gm[...],
    )


def weight_first_kernel(*refs):
    w1t, gain_in, acc, edge_acc, gain_acc = refs[15:]
    for i, term in enumerate(weight_args(refs[:15])):
        acc[i] = term
    edge_acc[...] = mm(refs[9][...], w1t[:, 2 * L :])
    gain_acc[...] = gain_in[...]


def weight_kernel(*refs):
    w1t, gain_in, acc_in, edge_in, gain_acc_in, acc, edge_acc, gain_acc = refs[15:]
    for i, term in enumerate(weight_args(refs[:15])):
        acc[i] = acc_in[i] + term
    edge_acc[...] = edge_in[...] + mm(refs[9][...], w1t[:, 2 * L :])
    gain_acc[...] = gain_acc_in[...] + gain_in[...]


def weight_last_kernel(place, *refs):
    gain_in, acc_in, gain_acc_in, out = refs[15:]
    core = place[1] % 2
    terms = weight_args(refs[:15])
    for i, term in enumerate(terms):
        out[(i // 4) ^ core, (i % 4) * L : (i % 4 + 1) * L, :] = (acc_in[i] + term).astype(BF16)
    row = lax.broadcasted_iota(jnp.int32, (L, L), 0)
    gain = gain_acc_in[...] + gain_in[...]
    out[1 ^ core, 3 * L :, :] = jnp.where(row == 0, gain, 0.0).astype(BF16)


def edge_last_kernel(gpe, w1t, edge_in, out):
    out[...] = edge_in[...] + mm(gpe[...], w1t[:, 2 * L :])


def node_last_kernel(own, p0, p1, p2, p3, spread, out):
    out[...] = landed(own, spread, p0, p1, p2, p3)


def finish_kernel(factor, place, mine, other, edge_in, edge_out, node_in, node_out, gain):
    core = place[1] % 2

    def half(index, lo, hi):
        a = mine[lo:hi].astype(F32)
        b = other[lo:hi].astype(F32)
        return jnp.where(core == index, a, b) * factor

    edge_in[...] = half(0, 0, 3 * L)
    edge_out[...] = half(0, 3 * L, 4 * L)
    node_in[...] = half(1, 0, 2 * L)
    node_out[...] = half(1, 2 * L, 3 * L)
    gain[...] = half(1, 3 * L, 3 * L + 8)


def even_pairs(size):
    return [(i, i ^ 1) for i in range(size)]


def odd_pairs(size):
    up = [((i + 1) % size, (i + 2) % size) for i in range(0, size, 2)]
    return up + [(b, a) for a, b in up]


def exchange(parts):
    slabs = lax.axis_size(SLAB)
    regions = lax.axis_size(REGION)
    return [
        lax.ppermute(parts[0], REGION, odd_pairs(regions)),
        lax.ppermute(parts[1], REGION, even_pairs(regions)),
        lax.ppermute(parts[2], SLAB, odd_pairs(slabs)),
        lax.ppermute(parts[3], SLAB, even_pairs(slabs)),
    ]


def reduce_all(payload):
    keep = payload[0].astype(F32)
    got = lax.ppermute(payload[1], "c", [(0, 1), (1, 0)])
    part = (keep + got.astype(F32)).astype(BF16).reshape(CHUNKS, CHUNK_ROWS, L)
    part = lax.all_to_all(part, PLANE, 0, 0, tiled=True)
    part = jnp.sum(part.astype(F32), axis=0).astype(BF16)
    deep = lax.axis_size("z")
    part = lax.all_to_all(jnp.broadcast_to(part[None], (deep,) + part.shape), "z", 0, 0, tiled=True)
    part = jnp.sum(part.astype(F32), axis=0).astype(BF16)
    part = jnp.broadcast_to(part[None], (CHUNKS,) + part.shape)
    mine = lax.all_to_all(part, PLANE, 0, 0, tiled=True).reshape(CHUNKS * CHUNK_ROWS, L)
    other = lax.ppermute(mine, "c", [(0, 1), (1, 0)])
    return mine, other


def local(
    nodes, feats, cotangent, edge_w1, edge_w2, node_w1, node_w2, ln_gain, senders, receivers, send_rows, edge_count
):
    edges = feats.shape[0]
    place = jnp.stack([lax.axis_index(REGION), lax.axis_index(SLAB)]).astype(jnp.int32)
    gain = ln_gain.reshape(1, L)
    halo_outs = [((HALO, L), BF16)] * 4
    *sends, spread = call(
        first_kernel, halo_outs + [((OWN, 4 * HALO), BF16)], place, nodes, send_rows, smem=1
    )
    t, tt, s, st, fw, w1t, w2t, n1t, n2t = call(
        prep_kernel,
        [
            ((edges, 2 * OWN), BF16), ((2 * OWN, edges), BF16), ((edges, OWN), BF16), ((OWN, edges), BF16),
            ((edges, L), F32), ((L, 3 * L), BF16), ((L, L), BF16), ((L, 2 * L), BF16), ((L, L), BF16),
        ],
        place, edge_count, senders.reshape(1, edges), receivers.reshape(1, edges), feats, edge_w1, edge_w2, node_w1, node_w2,
        smem=2,
    )
    h = nodes
    saved = []
    for _ in range(STEPS - 1):
        halo = exchange(sends)
        nxt, *rest = call(
            forward_kernel,
            [((OWN, L), BF16)] + halo_outs + [
                ((edges, L), F32), ((OWN, L), F32), ((OWN, L), BF16), ((OWN, L), F32), ((OWN, L), BF16),
                ((OWN, L), F32), ((OWN, 128), F32),
            ],
            h, *halo, t, s, st, fw, spread, edge_w1, edge_w2, node_w1, node_w2, gain,
        )
        saved.append((h, halo, rest[4:]))
        sends = rest[:4]
        h = nxt
    halo = exchange(sends)
    back_outs = [((OWN, L), F32)] + halo_outs + [
        ((edges, L), BF16), ((2 * OWN, L), F32), ((OWN, L), F32), ((OWN, L), BF16), ((OWN, L), BF16), ((OWN, L), BF16), ((1, L), F32),
    ]
    own, g0, g1, g2, g3, *rest = call(
        turn_kernel,
        back_outs + [((OWN, L), F32), ((OWN, L), BF16), ((OWN, L), BF16)],
        h, *halo, t, s, st, fw, edge_w1, edge_w2, node_w1, node_w2, gain, cotangent, tt, w1t, w2t, n1t, n2t,
    )
    back = exchange([g0, g1, g2, g3])
    *terms, gain_term, hidden_sum, summed, hidden_node = rest
    acc_outs = [((7, L, L), F32), ((edges, L), F32), ((1, L), F32)]
    totals = call(
        weight_first_kernel, acc_outs, h, *halo, feats, hidden_sum, summed, hidden_node, *terms, w1t, gain_term
    )
    for layer in reversed(range(STEPS - 1)):
        h, halo, (edge_slope, hidden_sum, summed, node_slope, hidden_node, normed, inv_dev) = saved[layer]
        own, g0, g1, g2, g3, *rest = call(
            backward_kernel, back_outs,
            own, *back, spread, edge_slope, node_slope, normed, inv_dev, gain, s, st, tt, w1t, w2t, n1t, n2t,
        )
        back = exchange([g0, g1, g2, g3])
        *terms, gain_term = rest
        shared = (h, *halo, feats, hidden_sum, summed, hidden_node, *terms)
        if layer > 0:
            totals = call(weight_kernel, acc_outs, *shared, w1t, gain_term, *totals)
    (payload,) = call(
        weight_last_kernel, [((2, 4 * L, L), BF16)], place, *shared, gain_term, totals[0], totals[2], smem=1
    )
    mine, other = reduce_all(payload)
    (edge_grad,) = call(edge_last_kernel, [((edges, L), F32)], terms[0], w1t, totals[1])
    (node_grad,) = call(node_last_kernel, [((OWN, L), F32)], own, *back, spread)
    devices = lax.axis_size(REGION) * lax.axis_size(SLAB)
    factor = float(OWN * devices) ** (-0.5)

    def finish(*refs):
        finish_kernel(factor, *refs)

    edge_in, edge_out, node_in, node_out, gain_grad = call(
        finish, [((3 * L, L), F32), ((L, L), F32), ((2 * L, L), F32), ((L, L), F32), ((8, L), F32)], place, mine, other, smem=1
    )
    return node_grad, edge_grad, edge_in, edge_out, node_in, node_out, gain_grad[0]


def solution(mesh):
    fine = Mesh(mesh.devices.reshape(4, 2, 8, 2, 2), AXES)
    split_rows = P(AXES, None)
    placed = (
        split_rows, split_rows, split_rows, P(), P(), P(), P(), P(), P(AXES), P(AXES), split_rows, P(REGION, SLAB),
    )
    return jax.shard_map(
        local,
        mesh=fine,
        in_specs=placed,
        out_specs=(split_rows, split_rows, P(), P(), P(), P(), P()),
        check_vma=False,
    )
```

```python
import jax
import jax.numpy as jnp
from jax import lax
from jax.experimental import pallas as pl
from jax.experimental.pallas import tpu as pltpu
from jax.sharding import Mesh
from jax.sharding import PartitionSpec as P

STEPS = 4
EPS = 1e-05
L = 256
OWN = 128
HALO = 32
BF16 = jnp.bfloat16
F32 = jnp.float32
AXES = ("x", "yh", "z", "yl", "c")
REGION = ("x", "yh")
SLAB = ("z", "yl", "c")
PLANE = ("x", "yh", "yl")
CHUNKS = 16
CHUNK_ROWS = 64


def mm(a, b):
    return jnp.dot(a, b, preferred_element_type=F32)


def mm_t(a, b):
    return lax.dot_general(a, b, (((0,), (0,)), ((), ())), preferred_element_type=F32)


def split(v):
    high = v.astype(BF16)
    low = (v - high.astype(F32)).astype(BF16)
    return high, low


def mm_split(v, w):
    high, low = split(v)
    return mm(high, w) + mm(low, w)


def sigmoid(v):
    return 0.5 * jnp.tanh(0.5 * v) + 0.5


def call(kernel, outs, *args, space=pltpu.VMEM, scalars=0, **kw):
    specs = [pl.BlockSpec(memory_space=pltpu.SMEM)] * scalars
    specs += [pl.BlockSpec(memory_space=space)] * (len(args) - scalars)
    if space is pltpu.HBM:
        args = args[:scalars] + tuple(pltpu.with_memory_space_constraint(a, space) for a in args[scalars:])
    return pl.pallas_call(
        kernel,
        out_shape=[jax.ShapeDtypeStruct(s, d) for s, d in outs],
        in_specs=specs,
        out_specs=[pl.BlockSpec(memory_space=pltpu.VMEM)] * len(outs),
        compiler_params=pltpu.CompilerParams(vmem_limit_bytes=32 * 1024 * 1024),
        **kw,
    )(*args)


def slot_lists(lists):
    slab_odd = lax.axis_index("c")
    region_odd = lax.axis_index("yh")
    a, b, c, d = (lists[i : i + 1, :] for i in range(4))
    return (
        jnp.where(region_odd == 1, d, c),
        jnp.where(region_odd == 1, c, d),
        jnp.where(slab_odd == 1, b, a),
        jnp.where(slab_odd == 1, a, b),
    )


def first_kernel(nodes, lists, s0, s1, s2, s3, spread, h, rows, sems):
    copies = [pltpu.make_async_copy(nodes, h, sems.at[0]), pltpu.make_async_copy(lists, rows, sems.at[1])]
    for copy in copies:
        copy.start()
    for copy in copies:
        copy.wait()
    row = lax.broadcasted_iota(jnp.int32, (OWN, HALO), 0)
    for i, (idx, out) in enumerate(zip(slot_lists(rows[...]), (s0, s1, s2, s3))):
        hot = (row == idx).astype(F32).astype(BF16)
        spread[:, i * HALO : (i + 1) * HALO] = hot
        out[...] = mm_t(hot, h[...]).astype(BF16)


def prep_kernel(
    count, send_in, recv_in, gain_in, w1_in, feats_in, n1_in, w2_in, n2_in, cot_in, nodes_in,
    t_out, tt_out, s_out, st_out, fw_out, w1t_out, w2t_out, n1t_out, n2t_out,
    gain_out, w1, feats, n1, w2, n2, cot, nodes,
    send_idx, recv_idx, gain, sems,
):
    pairs = (
        (w1_in, w1), (feats_in, feats), (send_in, send_idx), (recv_in, recv_idx),
        (n1_in, n1), (w2_in, w2), (n2_in, n2), (nodes_in, nodes), (gain_in, gain), (cot_in, cot),
    )
    copies = [pltpu.make_async_copy(a, b, sems.at[i]) for i, (a, b) in enumerate(pairs)]
    for copy in copies:
        copy.start()
    for copy in copies:
        copy.wait()
    edges = feats.shape[0]
    lane = lax.broadcasted_iota(jnp.int32, (1, edges), 1)
    live = lane < count[0, 0]
    snd = send_idx[...].reshape(1, edges)
    off = snd - OWN
    slab_swap = jnp.where(lax.axis_index("c") == 1, 3 * HALO, 2 * HALO)
    region_swap = jnp.where(lax.axis_index("yh") == 1, 3 * HALO, 2 * HALO)
    flip = jnp.where(off < 2 * HALO, slab_swap, region_swap)
    snd = jnp.where(off >= 0, OWN + (off ^ flip), snd)
    snd = jnp.where(live, snd, -1)
    rcv = jnp.where(live, recv_idx[...].reshape(1, edges), -1)
    tt = (lax.broadcasted_iota(jnp.int32, (2 * OWN, edges), 0) == snd).astype(F32)
    st = (lax.broadcasted_iota(jnp.int32, (OWN, edges), 0) == rcv).astype(F32)
    tt_out[...] = tt.astype(BF16)
    st_out[...] = st.astype(BF16)
    t_out[...] = tt.T.astype(BF16)
    s_out[...] = st.T.astype(BF16)
    fw_out[...] = mm(feats[...], w1[2 * L :])
    w1t_out[...] = w1[...].T
    w2t_out[...] = w2[...].T
    n1t_out[...] = n1[...].T
    n2t_out[...] = n2[...].T
    gain_out[...] = gain[...].reshape(1, L)


def forward_body(h, halo, t, s, st, fw, edge_w1, edge_w2, node_w1, node_w2):
    extended = jnp.concatenate([h] + halo, axis=0)
    from_send = mm(t, extended).astype(BF16)
    from_recv = mm(s, h).astype(BF16)
    pre = mm(from_send, edge_w1[:L]) + mm(from_recv, edge_w1[L : 2 * L]) + fw
    sig = sigmoid(pre)
    silu = pre * sig
    edge_slope = sig + silu * (1.0 - sig)
    hidden_sum = mm(st, silu.astype(BF16))
    summed = mm_split(hidden_sum, edge_w2).astype(BF16)
    pre_node = mm(h, node_w1[:L]) + mm(summed, node_w1[L:])
    sig_n = sigmoid(pre_node)
    silu_n = pre_node * sig_n
    node_slope = sig_n + silu_n * (1.0 - sig_n)
    hidden_node = silu_n.astype(BF16)
    update = mm(hidden_node, node_w2)
    centre = update - jnp.mean(update, axis=-1, keepdims=True)
    inv_dev = lax.rsqrt(jnp.mean(centre * centre, axis=-1, keepdims=True) + EPS)
    normed = centre * inv_dev
    return edge_slope, hidden_sum, summed, node_slope, hidden_node, normed, inv_dev


def forward_kernel(
    h_ref, p0, p1, p2, p3, t, s, st, fw, spread, edge_w1, edge_w2, node_w1, node_w2, gain,
    h_out, s0, s1, s2, s3, edge_slope_o, hidden_sum_o, summed_o, node_slope_o, hidden_node_o, normed_o, inv_dev_o,
):
    h = h_ref[...]
    parts = forward_body(
        h, [p0[...], p1[...], p2[...], p3[...]], t[...], s[...], st[...], fw[...],
        edge_w1, edge_w2[...], node_w1, node_w2[...],
    )
    edge_slope, hidden_sum, summed, node_slope, hidden_node, normed, inv_dev = parts
    nxt = (h.astype(F32) + normed * gain[...]).astype(BF16)
    h_out[...] = nxt
    sent = mm_t(spread[...], nxt).astype(BF16)
    for i, out in enumerate((s0, s1, s2, s3)):
        out[...] = sent[i * HALO : (i + 1) * HALO]
    edge_slope_o[...] = edge_slope
    hidden_sum_o[...] = hidden_sum
    summed_o[...] = summed
    node_slope_o[...] = node_slope
    hidden_node_o[...] = hidden_node
    normed_o[...] = normed
    inv_dev_o[...] = jnp.broadcast_to(inv_dev, inv_dev_o.shape)


def backward_body(
    up, parts, gain, s, st, tt, w1t, w2t, n1t, n2t,
    own_out, g0, g1, g2, g3, gpe_o, q_o, r_o, gpn_o, gu_o, gm_o, gain_o,
):
    edge_slope, node_slope, normed, inv_dev = parts
    gain_o[...] = jnp.sum(up * normed, axis=0, keepdims=True)
    scaled = up * gain
    gu = inv_dev * (
        scaled
        - jnp.mean(scaled, axis=-1, keepdims=True)
        - normed * jnp.mean(scaled * normed, axis=-1, keepdims=True)
    )
    gu = gu.astype(BF16)
    gpn = (mm(gu, n2t) * node_slope).astype(BF16)
    gj = mm(gpn, n1t)
    own_out[...] = up + gj[:, :L]
    gm = gj[:, L:].astype(BF16)
    high, low = split(mm(gm, w2t))
    s2 = jnp.concatenate([s, s], axis=1)
    ghe = mm(s2, jnp.concatenate([high, low], axis=0))
    gpe = (ghe * edge_slope).astype(BF16)
    q = mm(tt, gpe)
    r = mm(st, gpe)
    ge = mm_split(q, w1t[:, :L])
    own_out[...] = own_out[...] + ge[:OWN] + mm_split(r, w1t[:, L : 2 * L])
    for i, out in enumerate((g0, g1, g2, g3)):
        out[...] = ge[OWN + i * HALO : OWN + (i + 1) * HALO].astype(BF16)
    gpe_o[...] = gpe
    q_o[...] = q
    r_o[...] = r
    gpn_o[...] = gpn
    gu_o[...] = gu
    gm_o[...] = gm


def landed(own, spread, p0, p1, p2, p3):
    parts = jnp.concatenate([p0[...], p1[...], p2[...], p3[...]], axis=0)
    return own[...] + mm(spread[...], parts)


def turn_kernel(
    h_ref, p0, p1, p2, p3, t, s, st, fw, edge_w1, edge_w2, node_w1, node_w2, gain,
    cot, tt, w1t, w2t, n1t, n2t,
    own_out, g0, g1, g2, g3, gpe_o, q_o, r_o, gpn_o, gu_o, gm_o, gain_o, hidden_sum_o, summed_o, hidden_node_o,
):
    st_v, s_v = st[...], s[...]
    parts = forward_body(
        h_ref[...], [p0[...], p1[...], p2[...], p3[...]], t[...], s_v, st_v, fw[...],
        edge_w1, edge_w2[...], node_w1, node_w2[...],
    )
    edge_slope, hidden_sum, summed, node_slope, hidden_node, normed, inv_dev = parts
    hidden_sum_o[...] = hidden_sum
    summed_o[...] = summed
    hidden_node_o[...] = hidden_node
    backward_body(
        cot[...], (edge_slope, node_slope, normed, inv_dev), gain[...],
        s_v, st_v, tt[...], w1t, w2t[...], n1t[...], n2t[...],
        own_out, g0, g1, g2, g3, gpe_o, q_o, r_o, gpn_o, gu_o, gm_o, gain_o,
    )


def backward_kernel(
    own, p0, p1, p2, p3, spread, edge_slope, node_slope, normed, inv_dev, gain,
    s, st, tt, w1t, w2t, n1t, n2t,
    own_out, g0, g1, g2, g3, gpe_o, q_o, r_o, gpn_o, gu_o, gm_o, gain_o,
):
    up = landed(own, spread, p0, p1, p2, p3)
    backward_body(
        up, (edge_slope[...], node_slope[...], normed[...], inv_dev[:, :1]), gain[...],
        s[...], st[...], tt[...], w1t, w2t[...], n1t[...], n2t[...],
        own_out, g0, g1, g2, g3, gpe_o, q_o, r_o, gpn_o, gu_o, gm_o, gain_o,
    )


def weight_terms(h, halo, feats, hidden_sum, summed, hidden_node, gpe, q, r, gpn, gu, gm):
    extended = jnp.concatenate([h] + halo, axis=0)
    q_high, q_low = split(q)
    r_high, r_low = split(r)
    h_high, h_low = split(hidden_sum)
    return (
        mm_t(extended, q_high) + mm_t(extended, q_low),
        mm_t(h, r_high) + mm_t(h, r_low),
        mm_t(feats, gpe),
        mm_t(h_high, gm) + mm_t(h_low, gm),
        mm_t(h, gpn),
        mm_t(summed, gpn),
        mm_t(hidden_node, gu),
    )


def weight_args(refs):
    (h_ref, p0, p1, p2, p3, feats, hidden_sum, summed, hidden_node, gpe, q, r, gpn, gu, gm) = refs
    return weight_terms(
        h_ref[...], [p0[...], p1[...], p2[...], p3[...]], feats[...], hidden_sum[...], summed[...],
        hidden_node[...], gpe[...], q[...], r[...], gpn[...], gu[...], gm[...],
    )


def weight_first_kernel(*refs):
    w1t, gain_in, acc, edge_acc, gain_acc = refs[15:]
    for i, term in enumerate(weight_args(refs[:15])):
        acc[i] = term
    edge_acc[...] = mm(refs[9][...], w1t[:, 2 * L :])
    gain_acc[...] = gain_in[...]


def weight_kernel(*refs):
    w1t, gain_in, acc_in, edge_in, gain_acc_in, acc, edge_acc, gain_acc = refs[15:]
    for i, term in enumerate(weight_args(refs[:15])):
        acc[i] = acc_in[i] + term
    edge_acc[...] = edge_in[...] + mm(refs[9][...], w1t[:, 2 * L :])
    gain_acc[...] = gain_acc_in[...] + gain_in[...]


def weight_last_kernel(*refs):
    gain_in, acc_in, gain_acc_in, out = refs[15:]
    core = lax.axis_index("c")
    terms = weight_args(refs[:15])
    for i, term in enumerate(terms):
        out[(i // 4) ^ core, (i % 4) * L : (i % 4 + 1) * L, :] = (acc_in[i] + term).astype(BF16)
    row = lax.broadcasted_iota(jnp.int32, (L, L), 0)
    gain = gain_acc_in[...] + gain_in[...]
    out[1 ^ core, 3 * L :, :] = jnp.where(row == 0, gain, 0.0).astype(BF16)


def edge_last_kernel(gpe, w1t, edge_in, out):
    out[...] = edge_in[...] + mm(gpe[...], w1t[:, 2 * L :])


def node_last_kernel(own, p0, p1, p2, p3, spread, out):
    out[...] = landed(own, spread, p0, p1, p2, p3)


def finish_kernel(factor, mine, other, edge_in, edge_out, node_in, node_out, gain):
    core = lax.axis_index("c")

    def half(index, lo, hi):
        a = mine[lo:hi].astype(F32)
        b = other[lo:hi].astype(F32)
        return jnp.where(core == index, a, b) * factor

    edge_in[...] = half(0, 0, 3 * L)
    edge_out[...] = half(0, 3 * L, 4 * L)
    node_in[...] = half(1, 0, 2 * L)
    node_out[...] = half(1, 2 * L, 3 * L)
    gain[...] = half(1, 3 * L, 3 * L + 8)[0]


def even_pairs(size):
    return [(i, i ^ 1) for i in range(size)]


def odd_pairs(size):
    up = [((i + 1) % size, (i + 2) % size) for i in range(0, size, 2)]
    return up + [(b, a) for a, b in up]


def exchange(parts):
    slabs = lax.axis_size(SLAB)
    regions = lax.axis_size(REGION)
    return [
        lax.ppermute(parts[0], REGION, odd_pairs(regions)),
        lax.ppermute(parts[1], REGION, even_pairs(regions)),
        lax.ppermute(parts[2], SLAB, odd_pairs(slabs)),
        lax.ppermute(parts[3], SLAB, even_pairs(slabs)),
    ]


def reduce_all(payload, back):
    keep = payload[0].astype(F32)
    got = lax.ppermute(payload[1], "c", [(0, 1), (1, 0)])
    part = (keep + got.astype(F32)).astype(BF16).reshape(CHUNKS, CHUNK_ROWS, L)
    part = lax.all_to_all(part, PLANE, 0, 0, tiled=True)
    part = jnp.sum(part.astype(F32), axis=0).astype(BF16)
    part, *back = lax.optimization_barrier((part, *back))
    deep = lax.axis_size("z")
    part = lax.all_to_all(jnp.broadcast_to(part[None], (deep,) + part.shape), "z", 0, 0, tiled=True)
    part = jnp.sum(part.astype(F32), axis=0).astype(BF16)
    part = jnp.broadcast_to(part[None], (CHUNKS,) + part.shape)
    mine = lax.all_to_all(part, PLANE, 0, 0, tiled=True).reshape(CHUNKS * CHUNK_ROWS, L)
    other = lax.ppermute(mine, "c", [(0, 1), (1, 0)])
    return mine, other, back


def local(
    nodes, feats, cotangent, edge_w1, edge_w2, node_w1, node_w2, ln_gain, senders, receivers, send_rows, edge_count
):
    edges = feats.shape[0]
    halo_outs = [((HALO, L), BF16)] * 4
    *sends, spread = call(
        first_kernel, halo_outs + [((OWN, 4 * HALO), BF16)], nodes, send_rows, space=pltpu.HBM,
        scratch_shapes=[pltpu.VMEM((OWN, L), BF16), pltpu.VMEM((4, HALO), jnp.int32), pltpu.SemaphoreType.DMA((2,))],
    )
    t, tt, s, st, fw, w1t, w2t, n1t, n2t, gain, edge_w1, feats, node_w1, edge_w2, node_w2, cotangent, nodes = call(
        prep_kernel,
        [
            ((edges, 2 * OWN), BF16), ((2 * OWN, edges), BF16), ((edges, OWN), BF16), ((OWN, edges), BF16),
            ((edges, L), F32), ((L, 3 * L), BF16), ((L, L), BF16), ((L, 2 * L), BF16), ((L, L), BF16),
            ((1, L), F32), ((3 * L, L), BF16), ((edges, L), BF16), ((2 * L, L), BF16), ((L, L), BF16), ((L, L), BF16),
            ((OWN, L), F32), ((OWN, L), BF16),
        ],
        edge_count, senders, receivers, ln_gain, edge_w1, feats, node_w1, edge_w2, node_w2, cotangent, nodes,
        space=pltpu.HBM,
        scalars=1,
        scratch_shapes=[
            pltpu.VMEM((edges,), jnp.int32), pltpu.VMEM((edges,), jnp.int32),
            pltpu.VMEM((L,), F32), pltpu.SemaphoreType.DMA((10,)),
        ],
    )
    h = nodes
    saved = []
    for _ in range(STEPS - 1):
        halo = exchange(sends)
        nxt, *rest = call(
            forward_kernel,
            [((OWN, L), BF16)] + halo_outs + [
                ((edges, L), F32), ((OWN, L), F32), ((OWN, L), BF16), ((OWN, L), F32), ((OWN, L), BF16),
                ((OWN, L), F32), ((OWN, 128), F32),
            ],
            h, *halo, t, s, st, fw, spread, edge_w1, edge_w2, node_w1, node_w2, gain,
        )
        saved.append((h, halo, rest[4:]))
        sends = rest[:4]
        h = nxt
    halo = exchange(sends)
    back_outs = [((OWN, L), F32)] + halo_outs + [
        ((edges, L), BF16), ((2 * OWN, L), F32), ((OWN, L), F32), ((OWN, L), BF16), ((OWN, L), BF16), ((OWN, L), BF16), ((1, L), F32),
    ]
    own, g0, g1, g2, g3, *rest = call(
        turn_kernel,
        back_outs + [((OWN, L), F32), ((OWN, L), BF16), ((OWN, L), BF16)],
        h, *halo, t, s, st, fw, edge_w1, edge_w2, node_w1, node_w2, gain, cotangent, tt, w1t, w2t, n1t, n2t,
    )
    back = exchange([g0, g1, g2, g3])
    *terms, gain_term, hidden_sum, summed, hidden_node = rest
    acc_outs = [((7, L, L), F32), ((edges, L), F32), ((1, L), F32)]
    totals = call(
        weight_first_kernel, acc_outs, h, *halo, feats, hidden_sum, summed, hidden_node, *terms, w1t, gain_term
    )
    for layer in reversed(range(STEPS - 1)):
        h, halo, (edge_slope, hidden_sum, summed, node_slope, hidden_node, normed, inv_dev) = saved[layer]
        own, g0, g1, g2, g3, *rest = call(
            backward_kernel, back_outs,
            own, *back, spread, edge_slope, node_slope, normed, inv_dev, gain, s, st, tt, w1t, w2t, n1t, n2t,
        )
        back = exchange([g0, g1, g2, g3])
        *terms, gain_term = rest
        shared = (h, *halo, feats, hidden_sum, summed, hidden_node, *terms)
        if layer > 0:
            totals = call(weight_kernel, acc_outs, *shared, w1t, gain_term, *totals)
    (payload,) = call(
        weight_last_kernel, [((2, 4 * L, L), BF16)], *shared, gain_term, totals[0], totals[2]
    )
    mine, other, back = reduce_all(payload, back)
    (edge_grad,) = call(edge_last_kernel, [((edges, L), F32)], terms[0], w1t, totals[1])
    (node_grad,) = call(node_last_kernel, [((OWN, L), F32)], own, *back, spread)
    devices = lax.axis_size(REGION) * lax.axis_size(SLAB)
    factor = float(OWN * devices) ** (-0.5)

    def finish(*refs):
        finish_kernel(factor, *refs)

    edge_in, edge_out, node_in, node_out, gain_grad = call(
        finish, [((3 * L, L), F32), ((L, L), F32), ((2 * L, L), F32), ((L, L), F32), ((L,), F32)], mine, other
    )
    return node_grad, edge_grad, edge_in, edge_out, node_in, node_out, gain_grad


def solution(mesh):
    fine = Mesh(mesh.devices.reshape(4, 2, 8, 2, 2), AXES)
    split_rows = P(AXES, None)
    placed = (
        split_rows, split_rows, split_rows, P(), P(), P(), P(), P(), P(AXES), P(AXES), split_rows, P(REGION, SLAB),
    )
    return jax.shard_map(
        local,
        mesh=fine,
        in_specs=placed,
        out_specs=(split_rows, split_rows, P(), P(), P(), P(), P()),
        check_vma=False,
    )
```

```python
import jax
import jax.numpy as jnp
from jax import lax
from jax.experimental import pallas as pl
from jax.experimental.pallas import tpu as pltpu
from jax.sharding import Mesh
from jax.sharding import PartitionSpec as P

STEPS = 4
EPS = 1e-05
L = 256
OWN = 128
HALO = 32
BF16 = jnp.bfloat16
F32 = jnp.float32
AXES = ("x", "yh", "z", "yl", "c")
REGION = ("x", "yh")
SLAB = ("z", "yl", "c")
PLANE = ("x", "yh", "yl")
CHUNK = 128
CHUNKS = 16
CHUNK_ROWS = 64


def mm(a, b):
    return jnp.dot(a, b, preferred_element_type=F32)


def mm_t(a, b):
    return lax.dot_general(a, b, (((0,), (0,)), ((), ())), preferred_element_type=F32)


def split(v):
    high = v.astype(BF16)
    low = (v - high.astype(F32)).astype(BF16)
    return high, low


def mm_split(v, w):
    high, low = split(v)
    return mm(high, w) + mm(low, w)


def sigmoid(v):
    return 0.5 * jnp.tanh(0.5 * v) + 0.5


def call(kernel, outs, *args, space=pltpu.VMEM, free=(), **kw):
    specs = [pl.BlockSpec(memory_space=pl.ANY if i in free else space) for i in range(len(args))]
    if space is pltpu.HBM:
        args = [a if i in free else pltpu.with_memory_space_constraint(a, space) for i, a in enumerate(args)]
    return pl.pallas_call(
        kernel,
        out_shape=[jax.ShapeDtypeStruct(s, d) for s, d in outs],
        in_specs=specs,
        out_specs=[pl.BlockSpec(memory_space=pltpu.VMEM)] * len(outs),
        compiler_params=pltpu.CompilerParams(vmem_limit_bytes=32 * 1024 * 1024),
        **kw,
    )(*args)


def slot_lists(lists):
    slab_odd = lax.axis_index("c")
    region_odd = lax.axis_index("yh")
    a, b, c, d = (lists[i : i + 1, :] for i in range(4))
    return (
        jnp.where(region_odd == 1, d, c),
        jnp.where(region_odd == 1, c, d),
        jnp.where(slab_odd == 1, b, a),
        jnp.where(slab_odd == 1, a, b),
    )


def first_kernel(nodes, lists, s0, s1, s2, s3, spread, h, rows, sems):
    copies = [pltpu.make_async_copy(nodes, h, sems.at[0]), pltpu.make_async_copy(lists, rows, sems.at[1])]
    for copy in copies:
        copy.start()
    for copy in copies:
        copy.wait()
    row = lax.broadcasted_iota(jnp.int32, (OWN, HALO), 0)
    for i, (idx, out) in enumerate(zip(slot_lists(rows[...]), (s0, s1, s2, s3))):
        hot = (row == idx).astype(F32).astype(BF16)
        spread[:, i * HALO : (i + 1) * HALO] = hot
        out[...] = mm_t(hot, h[...]).astype(BF16)


def prep_kernel(
    count_in, send_in, recv_in, gain_in, w1_in, feats_in, n1_in, w2_in, n2_in, cot_in, nodes_in, spread_in,
    tos_out, th_out, ss_out, ttst_out, st_out, st_sent_out, pre_out, fw_out, w1t_out, back_out, n2t_out, mix_out,
    gain_out, w1, feats, n1, w2, n2, cot, nodes,
    spread, count, send_idx, recv_idx, gain, sems,
):
    pairs = (
        (w1_in, w1), (feats_in, feats), (count_in, count), (spread_in, spread), (send_in, send_idx), (recv_in, recv_idx),
        (n1_in, n1), (w2_in, w2), (n2_in, n2), (nodes_in, nodes), (gain_in, gain), (cot_in, cot),
    )
    copies = [pltpu.make_async_copy(a, b, sems.at[i]) for i, (a, b) in enumerate(pairs)]
    for copy in copies:
        copy.start()
    for copy in copies:
        copy.wait()
    edges = feats.shape[0]
    lane = lax.broadcasted_iota(jnp.int32, (1, edges), 1)
    live = lane < count[0, 0]
    snd = send_idx[...].reshape(1, edges)
    off = snd - OWN
    slab_swap = jnp.where(lax.axis_index("c") == 1, 3 * HALO, 2 * HALO)
    region_swap = jnp.where(lax.axis_index("yh") == 1, 3 * HALO, 2 * HALO)
    flip = jnp.where(off < 2 * HALO, slab_swap, region_swap)
    snd = jnp.where(off >= 0, OWN + (off ^ flip), snd)
    snd = jnp.where(live, snd, -1)
    rcv = jnp.where(live, recv_idx[...].reshape(1, edges), -1)
    tt = (lax.broadcasted_iota(jnp.int32, (2 * OWN, edges), 0) == snd).astype(F32)
    st = (lax.broadcasted_iota(jnp.int32, (OWN, edges), 0) == rcv).astype(F32)
    spread_t = spread[...].T
    tt16 = tt.astype(BF16)
    st16 = st.astype(BF16)
    t16 = tt.T.astype(BF16)
    s16 = st.T.astype(BF16)
    ttst_out[: 2 * OWN] = tt16
    ttst_out[2 * OWN :] = st16
    st_out[...] = st16
    st_sent_out[...] = mm(spread_t, st16).astype(BF16)
    for i in range(2):
        tos_out[:, i * OWN : (i + 1) * OWN] = t16[:, :OWN]
        th_out[:, i * OWN : (i + 1) * OWN] = t16[:, OWN:]
        tos_out[:, (2 + i) * OWN : (3 + i) * OWN] = s16
        ss_out[:, i * OWN : (i + 1) * OWN] = s16
    fw_out[...] = mm(feats[...], w1[2 * L :])
    own_pre(nodes[...], tos_out, fw_out, w1, pre_out)
    w1t_out[...] = w1[...].T
    n2t_out[...] = n2[...].T
    mix_high, mix_low = split(mm(w2[...], n1[L:]))
    mix_out[:, :L] = mix_high
    mix_out[:, L:] = mix_low
    back_out[:, : 2 * L] = n1[...].T
    back_out[:, 2 * L : 3 * L] = mix_high.T
    back_out[:, 3 * L :] = mix_low.T
    gain_out[...] = gain[...].reshape(1, L)


def edge_hidden(halo, th, pre_part, edge_w1, keep):
    high, low = split(mm(jnp.concatenate(halo, axis=0), edge_w1[:L]))
    table = jnp.concatenate([high, low], axis=0)
    hidden = []
    for lo in range(0, pre_part.shape[0], CHUNK):
        pre = mm(th[lo : lo + CHUNK], table) + pre_part[lo : lo + CHUNK]
        hidden.append(keep(lo, pre))
    return jnp.concatenate(hidden, axis=0)


def edge_slopes(pre):
    sig = sigmoid(pre)
    silu = pre * sig
    return silu, sig + silu * (1.0 - sig)


def node_body(h, hidden_sum, node_w1, mix, node_w2):
    high, low = split(hidden_sum)
    pre_node = mm(h, node_w1[:L]) + mm(high, mix[:, :L]) + mm(high, mix[:, L:]) + mm(low, mix[:, :L])
    silu_n, node_slope = edge_slopes(pre_node)
    hidden_node = silu_n.astype(BF16)
    update = mm(hidden_node, node_w2[...])
    centre = update - jnp.mean(update, axis=-1, keepdims=True)
    inv_dev = lax.rsqrt(jnp.mean(centre * centre, axis=-1, keepdims=True) + EPS)
    return node_slope, hidden_node, centre * inv_dev, inv_dev


def own_pre(h, tos, fw, edge_w1, out):
    far_high, far_low = split(mm(h, edge_w1[:L]))
    near_high, near_low = split(mm(h, edge_w1[L : 2 * L]))
    table = jnp.concatenate([far_high, far_low, near_high, near_low], axis=0)
    for lo in range(0, fw.shape[0], CHUNK):
        out[lo : lo + CHUNK] = mm(tos[lo : lo + CHUNK], table) + fw[lo : lo + CHUNK]


def forward_kernel(
    p0, p1, p2, p3, q0, q1, q2, q3, pre_part, th, st_sent, edge_w1, node_w1, mix, node_w2, gain,
    s0, s1, s2, s3, pre_o, hidden_o,
):
    def keep(lo, pre):
        pre_o[lo : lo + CHUNK] = pre
        part = (pre * sigmoid(pre)).astype(BF16)
        hidden_o[lo : lo + CHUNK] = part
        return part

    hidden = edge_hidden([p0[...], p1[...], p2[...], p3[...]], th, pre_part, edge_w1, keep)
    h = jnp.concatenate([q0[...], q1[...], q2[...], q3[...]], axis=0)
    normed = node_body(h, mm(st_sent[...], hidden), node_w1, mix, node_w2)[2]
    sent = (h.astype(F32) + normed * gain[...]).astype(BF16)
    for i, out in enumerate((s0, s1, s2, s3)):
        out[...] = sent[i * HALO : (i + 1) * HALO]


def own_kernel(
    h_ref, pre, hidden, st, tos, fw, edge_w1, node_w1, mix, node_w2, gain,
    h_out, pre_part_o, edge_slope_o, hidden_sum_o, node_slope_o, hidden_node_o, normed_o, inv_dev_o,
):
    h = h_ref[...]
    hidden_sum = mm(st[...], hidden[...])
    node_slope, hidden_node, normed, inv_dev = node_body(h, hidden_sum, node_w1, mix, node_w2)
    nxt = (h.astype(F32) + normed * gain[...]).astype(BF16)
    h_out[...] = nxt
    own_pre(nxt, tos, fw, edge_w1, pre_part_o)
    edge_slope_o[...] = edge_slopes(pre[...])[1]
    hidden_sum_o[...] = hidden_sum
    node_slope_o[...] = node_slope
    hidden_node_o[...] = hidden_node
    normed_o[...] = normed
    inv_dev_o[...] = jnp.broadcast_to(inv_dev, inv_dev_o.shape)


def backward_body(
    up, parts, gain, ss, ttst, w1t, back, n2t, g0, g1, g2, g3, gpe_o, qr_o, gpn_o, gu_o, gain_o
):
    edge_slope, node_slope, normed, inv_dev = parts
    gain_o[...] = jnp.sum(up * normed, axis=0, keepdims=True)
    scaled = up * gain
    gu = inv_dev * (
        scaled
        - jnp.mean(scaled, axis=-1, keepdims=True)
        - normed * jnp.mean(scaled * normed, axis=-1, keepdims=True)
    )
    gu = gu.astype(BF16)
    gpn = (mm(gu, n2t[...]) * node_slope).astype(BF16)
    gu_o[...] = gu
    gpn_o[...] = gpn
    gh = mm(gpn, back[:, 2 * L : 3 * L]) + mm(gpn, back[:, 3 * L :])
    high, low = split(gh)
    pair = jnp.concatenate([high, low], axis=0)
    gpe = []
    for lo in range(0, edge_slope.shape[0], CHUNK):
        part = (mm(ss[lo : lo + CHUNK], pair) * edge_slope[lo : lo + CHUNK]).astype(BF16)
        gpe_o[lo : lo + CHUNK] = part
        gpe.append(part)
    qr = mm(ttst[...], jnp.concatenate(gpe, axis=0))
    q_high, q_low = split(qr[OWN : 2 * OWN])
    far = w1t[:, :L]
    ge = mm(q_high, far) + mm(q_low, far)
    for i, out in enumerate((g0, g1, g2, g3)):
        out[...] = ge[i * HALO : (i + 1) * HALO].astype(BF16)
    qr_o[...] = qr


def rest_kernel(up, qr, gpn, w1t, back, own_out):
    q_high, q_low = split(qr[:OWN])
    r_high, r_low = split(qr[2 * OWN :])
    far, near = w1t[:, :L], w1t[:, L : 2 * L]
    own_out[...] = (
        up[...] + mm(gpn[...], back[:, :L]) + mm(q_high, far) + mm(q_low, far) + mm(r_high, near) + mm(r_low, near)
    )


def landed(own, spread, p0, p1, p2, p3):
    parts = jnp.concatenate([p0[...], p1[...], p2[...], p3[...]], axis=0)
    return own[...] + mm(spread[...], parts)


def turn_kernel(
    h_ref, p0, p1, p2, p3, pre_part, th, st, edge_w1, node_w1, mix, node_w2, gain, cot, ss, ttst, w1t, back, n2t,
    g0, g1, g2, g3, gpe_o, qr_o, gpn_o, gu_o, gain_o, hidden_sum_o, hidden_node_o, edge_slope,
):
    def keep(lo, pre):
        silu, slope = edge_slopes(pre)
        edge_slope[lo : lo + CHUNK] = slope
        return silu.astype(BF16)

    hidden = edge_hidden([p0[...], p1[...], p2[...], p3[...]], th, pre_part, edge_w1, keep)
    hidden_sum = mm(st[...], hidden)
    node_slope, hidden_node, normed, inv_dev = node_body(h_ref[...], hidden_sum, node_w1, mix, node_w2)
    hidden_sum_o[...] = hidden_sum
    hidden_node_o[...] = hidden_node
    backward_body(
        cot[...], (edge_slope, node_slope, normed, inv_dev), gain[...], ss, ttst, w1t, back, n2t,
        g0, g1, g2, g3, gpe_o, qr_o, gpn_o, gu_o, gain_o,
    )


def backward_kernel(
    own, p0, p1, p2, p3, spread, edge_slope, node_slope, normed, inv_dev, gain, ss, ttst, w1t, back, n2t,
    g0, g1, g2, g3, gpe_o, qr_o, gpn_o, gu_o, gain_o, up_o,
):
    up = landed(own, spread, p0, p1, p2, p3)
    up_o[...] = up
    backward_body(
        up, (edge_slope, node_slope[...], normed[...], inv_dev[:, :1]), gain[...], ss, ttst, w1t, back, n2t,
        g0, g1, g2, g3, gpe_o, qr_o, gpn_o, gu_o, gain_o,
    )


def weight_args(refs):
    h_ref, p0, p1, p2, p3, feats, edge_w2, hidden_sum, hidden_node, back, gpe, qr, gpn, gu = refs
    gm = mm(gpn[...], back[:, L : 2 * L]).astype(BF16)
    h = h_ref[...]
    extended = jnp.concatenate([h, p0[...], p1[...], p2[...], p3[...]], axis=0)
    qr_high, qr_low = split(qr[...])
    h_high, h_low = split(hidden_sum[...])
    summed = (mm(h_high, edge_w2[...]) + mm(h_low, edge_w2[...])).astype(BF16)
    return (
        mm_t(extended, qr_high[: 2 * OWN]) + mm_t(extended, qr_low[: 2 * OWN]),
        mm_t(h, qr_high[2 * OWN :]) + mm_t(h, qr_low[2 * OWN :]),
        mm_t(feats[...], gpe[...]),
        mm_t(h_high, gm) + mm_t(h_low, gm),
        mm_t(h, gpn[...]),
        mm_t(summed, gpn[...]),
        mm_t(hidden_node[...], gu[...]),
    )


def weight_first_kernel(*refs):
    w1t, gain_in, acc, edge_acc, gain_acc = refs[14:]
    for i, term in enumerate(weight_args(refs[:14])):
        acc[i] = term
    edge_acc[...] = mm(refs[10][...], w1t[:, 2 * L :])
    gain_acc[...] = gain_in[...]


def weight_kernel(*refs):
    w1t, gain_in, acc_in, edge_in, gain_acc_in, acc, edge_acc, gain_acc = refs[14:]
    for i, term in enumerate(weight_args(refs[:14])):
        acc[i] = acc_in[i] + term
    edge_acc[...] = edge_in[...] + mm(refs[10][...], w1t[:, 2 * L :])
    gain_acc[...] = gain_acc_in[...] + gain_in[...]


def weight_last_kernel(*refs):
    gain_in, acc_in, gain_acc_in, out = refs[14:]
    core = lax.axis_index("c")
    terms = weight_args(refs[:14])
    for i, term in enumerate(terms):
        out[(i // 4) ^ core, (i % 4) * L : (i % 4 + 1) * L, :] = (acc_in[i] + term).astype(BF16)
    row = lax.broadcasted_iota(jnp.int32, (L, L), 0)
    gain = gain_acc_in[...] + gain_in[...]
    out[1 ^ core, 3 * L :, :] = jnp.where(row == 0, gain, 0.0).astype(BF16)


def edge_last_kernel(gpe, w1t, edge_in, out):
    out[...] = edge_in[...] + mm(gpe[...], w1t[:, 2 * L :])


def node_last_kernel(own, p0, p1, p2, p3, spread, out):
    out[...] = landed(own, spread, p0, p1, p2, p3)


def finish_kernel(factor, mine, other, edge_in, edge_out, node_in, node_out, gain):
    core = lax.axis_index("c")

    def half(index, lo, hi):
        a = mine[lo:hi].astype(F32)
        b = other[lo:hi].astype(F32)
        return jnp.where(core == index, a, b) * factor

    edge_in[...] = half(0, 0, 3 * L)
    edge_out[...] = half(0, 3 * L, 4 * L)
    node_in[...] = half(1, 0, 2 * L)
    node_out[...] = half(1, 2 * L, 3 * L)
    gain[...] = half(1, 3 * L, 3 * L + 8)[0]


def even_pairs(size):
    return [(i, i ^ 1) for i in range(size)]


def odd_pairs(size):
    up = [((i + 1) % size, (i + 2) % size) for i in range(0, size, 2)]
    return up + [(b, a) for a, b in up]


def exchange(parts):
    slabs = lax.axis_size(SLAB)
    regions = lax.axis_size(REGION)
    return [
        lax.ppermute(parts[0], REGION, odd_pairs(regions)),
        lax.ppermute(parts[1], REGION, even_pairs(regions)),
        lax.ppermute(parts[2], SLAB, odd_pairs(slabs)),
        lax.ppermute(parts[3], SLAB, even_pairs(slabs)),
    ]


def reduce_all(payload, back):
    keep = payload[0].astype(F32)
    got = lax.ppermute(payload[1], "c", [(0, 1), (1, 0)])
    part = (keep + got.astype(F32)).astype(BF16).reshape(CHUNKS, CHUNK_ROWS, L)
    part = lax.all_to_all(part, PLANE, 0, 0, tiled=True)
    part = jnp.sum(part.astype(F32), axis=0).astype(BF16)
    deep = lax.axis_size("z")
    part = lax.all_to_all(jnp.broadcast_to(part[None], (deep,) + part.shape), "z", 0, 0, tiled=True)
    part = jnp.sum(part.astype(F32), axis=0).astype(BF16)
    part, *back = lax.optimization_barrier((part, *back))
    part = jnp.broadcast_to(part[None], (CHUNKS,) + part.shape)
    mine = lax.all_to_all(part, PLANE, 0, 0, tiled=True).reshape(CHUNKS * CHUNK_ROWS, L)
    other = lax.ppermute(mine, "c", [(0, 1), (1, 0)])
    return mine, other, back


def local(
    nodes, feats, cotangent, edge_w1, edge_w2, node_w1, node_w2, ln_gain, senders, receivers, send_rows, edge_count
):
    edges = feats.shape[0]
    halo_outs = [((HALO, L), BF16)] * 4
    *sends, spread = call(
        first_kernel, halo_outs + [((OWN, 4 * HALO), BF16)], nodes, send_rows, space=pltpu.HBM,
        scratch_shapes=[pltpu.VMEM((OWN, L), BF16), pltpu.VMEM((4, HALO), jnp.int32), pltpu.SemaphoreType.DMA((2,))],
    )
    tos, th, ss, ttst, st, st_sent, pre_part, fw, w1t, back_w, n2t, mix, gain, edge_w1, feats, node_w1, edge_w2, node_w2, cotangent, nodes = call(
        prep_kernel,
        [
            ((edges, 4 * OWN), BF16), ((edges, 2 * OWN), BF16), ((edges, 2 * OWN), BF16), ((3 * OWN, edges), BF16),
            ((OWN, edges), BF16), ((OWN, edges), BF16), ((edges, L), F32),
            ((edges, L), F32), ((L, 3 * L), BF16), ((L, 4 * L), BF16), ((L, L), BF16), ((L, 2 * L), BF16),
            ((1, L), F32), ((3 * L, L), BF16), ((edges, L), BF16), ((2 * L, L), BF16), ((L, L), BF16), ((L, L), BF16),
            ((OWN, L), F32), ((OWN, L), BF16),
        ],
        edge_count, senders, receivers, ln_gain, edge_w1, feats, node_w1, edge_w2, node_w2, cotangent, nodes, spread,
        space=pltpu.HBM,
        free=(0, 11),
        scratch_shapes=[
            pltpu.VMEM((OWN, 4 * HALO), BF16), pltpu.SMEM((1, 1), jnp.int32),
            pltpu.VMEM((edges,), jnp.int32), pltpu.VMEM((edges,), jnp.int32),
            pltpu.VMEM((L,), F32), pltpu.SemaphoreType.DMA((12,)),
        ],
    )
    h = nodes
    saved = []
    for _ in range(STEPS - 1):
        halo = exchange(sends)
        *sends, pre, hidden = call(
            forward_kernel,
            halo_outs + [((edges, L), F32), ((edges, L), BF16)],
            *halo, *sends, pre_part, th, st_sent, edge_w1, node_w1, mix, node_w2, gain,
        )
        nxt, pre_part, *rest = call(
            own_kernel,
            [
                ((OWN, L), BF16), ((edges, L), F32), ((edges, L), F32), ((OWN, L), F32), ((OWN, L), F32), ((OWN, L), BF16),
                ((OWN, L), F32), ((OWN, 128), F32),
            ],
            h, pre, hidden, st, tos, fw, edge_w1, node_w1, mix, node_w2, gain,
        )
        saved.append((h, halo, rest))
        h = nxt
    halo = exchange(sends)
    back_outs = halo_outs + [
        ((edges, L), BF16), ((3 * OWN, L), F32), ((OWN, L), BF16), ((OWN, L), BF16), ((1, L), F32),
    ]
    g0, g1, g2, g3, *terms, gain_term, hidden_sum, hidden_node = call(
        turn_kernel,
        back_outs + [((OWN, L), F32), ((OWN, L), BF16)],
        h, *halo, pre_part, th, st, edge_w1, node_w1, mix, node_w2, gain, cotangent, ss, ttst, w1t, back_w, n2t,
        scratch_shapes=[pltpu.VMEM((edges, L), F32)],
    )
    back = exchange([g0, g1, g2, g3])
    own_out = [((OWN, L), F32)]
    (own,) = call(rest_kernel, own_out, cotangent, terms[1], terms[2], w1t, back_w)
    acc_outs = [((7, L, L), F32), ((edges, L), F32), ((1, L), F32)]
    totals = call(
        weight_first_kernel, acc_outs, h, *halo, feats, edge_w2, hidden_sum, hidden_node, back_w, *terms, w1t, gain_term
    )
    for layer in reversed(range(STEPS - 1)):
        h, halo, (edge_slope, hidden_sum, node_slope, hidden_node, normed, inv_dev) = saved[layer]
        g0, g1, g2, g3, *terms, gain_term, up = call(
            backward_kernel, back_outs + own_out,
            own, *back, spread, edge_slope, node_slope, normed, inv_dev, gain, ss, ttst, w1t, back_w, n2t,
        )
        back = exchange([g0, g1, g2, g3])
        (own,) = call(rest_kernel, own_out, up, terms[1], terms[2], w1t, back_w)
        shared = (h, *halo, feats, edge_w2, hidden_sum, hidden_node, back_w, *terms)
        if layer > 0:
            totals = call(weight_kernel, acc_outs, *shared, w1t, gain_term, *totals)
    (payload,) = call(
        weight_last_kernel, [((2, 4 * L, L), BF16)], *shared, gain_term, totals[0], totals[2]
    )
    mine, other, back = reduce_all(payload, back)
    (edge_grad,) = call(edge_last_kernel, [((edges, L), F32)], terms[0], w1t, totals[1])
    (node_grad,) = call(node_last_kernel, [((OWN, L), F32)], own, *back, spread)
    devices = lax.axis_size(REGION) * lax.axis_size(SLAB)
    factor = float(OWN * devices) ** (-0.5)

    def finish(*refs):
        finish_kernel(factor, *refs)

    edge_in, edge_out, node_in, node_out, gain_grad = call(
        finish, [((3 * L, L), F32), ((L, L), F32), ((2 * L, L), F32), ((L, L), F32), ((L,), F32)], mine, other
    )
    return node_grad, edge_grad, edge_in, edge_out, node_in, node_out, gain_grad


def solution(mesh):
    fine = Mesh(mesh.devices.reshape(4, 2, 8, 2, 2), AXES)
    split_rows = P(AXES, None)
    placed = (
        split_rows, split_rows, split_rows, P(), P(), P(), P(), P(), P(AXES), P(AXES), split_rows, P(REGION, SLAB),
    )
    return jax.shard_map(
        local,
        mesh=fine,
        in_specs=placed,
        out_specs=(split_rows, split_rows, P(), P(), P(), P(), P()),
        check_vma=False,
    )
```

```python
import functools

import jax
import jax.numpy as jnp
from jax import lax
from jax.experimental import pallas as pl
from jax.experimental.pallas import tpu as pltpu
from jax.sharding import Mesh
from jax.sharding import PartitionSpec as P

STEPS = 4
EPS = 1e-05
L = 256
OWN = 128
HALO = 32
BF16 = jnp.bfloat16
F32 = jnp.float32
AXES = ("x", "yh", "z", "yl", "c")
REGION = ("x", "yh")
SLAB = ("z", "yl", "c")
PLANE = ("x", "yh", "yl")
CHUNK = 128
CHUNKS = 16
CHUNK_ROWS = 64


def mm(a, b):
    return jnp.dot(a, b, preferred_element_type=F32)


def mm_t(a, b):
    return lax.dot_general(a, b, (((0,), (0,)), ((), ())), preferred_element_type=F32)


def split(v):
    high = v.astype(BF16)
    low = (v - high.astype(F32)).astype(BF16)
    return high, low


def mm_split(v, w):
    high, low = split(v)
    return mm(high, w) + mm(low, w)


def sigmoid(v):
    return 0.5 * jnp.tanh(0.5 * v) + 0.5


def call(kernel, outs, *args, space=pltpu.VMEM, free=(), **kw):
    specs = [pl.BlockSpec(memory_space=pl.ANY if i in free else space) for i in range(len(args))]
    if space is pltpu.HBM:
        args = [a if i in free else pltpu.with_memory_space_constraint(a, space) for i, a in enumerate(args)]
    return pl.pallas_call(
        kernel,
        out_shape=[jax.ShapeDtypeStruct(s, d) for s, d in outs],
        in_specs=specs,
        out_specs=[pl.BlockSpec(memory_space=pltpu.VMEM)] * len(outs),
        compiler_params=pltpu.CompilerParams(vmem_limit_bytes=32 * 1024 * 1024),
        **kw,
    )(*args)


def slot_lists(lists):
    slab_odd = lax.axis_index("c")
    region_odd = lax.axis_index("yh")
    a, b, c, d = (lists[i : i + 1, :] for i in range(4))
    return (
        jnp.where(region_odd == 1, d, c),
        jnp.where(region_odd == 1, c, d),
        jnp.where(slab_odd == 1, b, a),
        jnp.where(slab_odd == 1, a, b),
    )


def first_kernel(nodes, lists, s0, s1, s2, s3, spread, h, rows, sems):
    copies = [pltpu.make_async_copy(nodes, h, sems.at[0]), pltpu.make_async_copy(lists, rows, sems.at[1])]
    for copy in copies:
        copy.start()
    for copy in copies:
        copy.wait()
    row = lax.broadcasted_iota(jnp.int32, (OWN, HALO), 0)
    for i, (idx, out) in enumerate(zip(slot_lists(rows[...]), (s0, s1, s2, s3))):
        hot = (row == idx).astype(F32).astype(BF16)
        spread[:, i * HALO : (i + 1) * HALO] = hot
        out[...] = mm_t(hot, h[...]).astype(BF16)


def prep_kernel(
    count_in, send_in, recv_in, gain_in, w1_in, feats_in, n1_in, w2_in, n2_in, cot_in, nodes_in, spread_in,
    tos_out, th_out, ss_out, ttst_out, st_out, st_sent_out, pre_out, fw_out, w1t_out, back_out, n2t_out, mix_out,
    gain_out, w1, feats, n1, w2, n2, cot, nodes,
    spread, count, send_idx, recv_idx, gain, sems,
):
    pairs = (
        (w1_in, w1), (feats_in, feats), (count_in, count), (spread_in, spread), (send_in, send_idx), (recv_in, recv_idx),
        (n1_in, n1), (w2_in, w2), (n2_in, n2), (nodes_in, nodes), (gain_in, gain), (cot_in, cot),
    )
    copies = [pltpu.make_async_copy(a, b, sems.at[i]) for i, (a, b) in enumerate(pairs)]
    for copy in copies:
        copy.start()
    for copy in copies:
        copy.wait()
    edges = feats.shape[0]
    lane = lax.broadcasted_iota(jnp.int32, (1, edges), 1)
    live = lane < count[0, 0]
    snd = send_idx[...].reshape(1, edges)
    off = snd - OWN
    slab_swap = jnp.where(lax.axis_index("c") == 1, 3 * HALO, 2 * HALO)
    region_swap = jnp.where(lax.axis_index("yh") == 1, 3 * HALO, 2 * HALO)
    flip = jnp.where(off < 2 * HALO, slab_swap, region_swap)
    snd = jnp.where(off >= 0, OWN + (off ^ flip), snd)
    snd = jnp.where(live, snd, -1)
    rcv = jnp.where(live, recv_idx[...].reshape(1, edges), -1)
    tt = (lax.broadcasted_iota(jnp.int32, (2 * OWN, edges), 0) == snd).astype(F32)
    st = (lax.broadcasted_iota(jnp.int32, (OWN, edges), 0) == rcv).astype(F32)
    spread_t = spread[...].T
    tt16 = tt.astype(BF16)
    st16 = st.astype(BF16)
    t16 = tt.T.astype(BF16)
    s16 = st.T.astype(BF16)
    ttst_out[: 2 * OWN] = tt16
    ttst_out[2 * OWN :] = st16
    st_out[...] = st16
    st_sent_out[...] = mm(spread_t, st16).astype(BF16)
    for i in range(2):
        tos_out[:, i * OWN : (i + 1) * OWN] = t16[:, :OWN]
        th_out[:, i * OWN : (i + 1) * OWN] = t16[:, OWN:]
        tos_out[:, (2 + i) * OWN : (3 + i) * OWN] = s16
        ss_out[:, i * OWN : (i + 1) * OWN] = s16
    fw_out[...] = mm(feats[...], w1[2 * L :])
    own_pre(nodes[...], tos_out, fw_out, w1, pre_out)
    w1t_out[...] = w1[...].T
    n2t_out[...] = n2[...].T
    mix_high, mix_low = split(mm(w2[...], n1[L:]))
    mix_out[:, :L] = mix_high
    mix_out[:, L:] = mix_low
    back_out[:, : 2 * L] = n1[...].T
    back_out[:, 2 * L : 3 * L] = mix_high.T
    back_out[:, 3 * L :] = mix_low.T
    gain_out[...] = gain[...].reshape(1, L)


def edge_hidden(halo, th, pre_part, edge_w1, keep):
    high, low = split(mm(jnp.concatenate(halo, axis=0), edge_w1[:L]))
    table = jnp.concatenate([high, low], axis=0)
    hidden = []
    for lo in range(0, pre_part.shape[0], CHUNK):
        pre = mm(th[lo : lo + CHUNK], table) + pre_part[lo : lo + CHUNK]
        hidden.append(keep(lo, pre))
    return jnp.concatenate(hidden, axis=0)


def edge_slopes(pre):
    sig = sigmoid(pre)
    silu = pre * sig
    return silu, sig + silu * (1.0 - sig)


def node_body(h, hidden_sum, node_w1, mix, node_w2):
    high, low = split(hidden_sum)
    pre_node = mm(h, node_w1[:L]) + mm(high, mix[:, :L]) + mm(high, mix[:, L:]) + mm(low, mix[:, :L])
    silu_n, node_slope = edge_slopes(pre_node)
    hidden_node = silu_n.astype(BF16)
    update = mm(hidden_node, node_w2[...])
    centre = update - jnp.mean(update, axis=-1, keepdims=True)
    inv_dev = lax.rsqrt(jnp.mean(centre * centre, axis=-1, keepdims=True) + EPS)
    return node_slope, hidden_node, centre * inv_dev, inv_dev


def own_pre(h, tos, fw, edge_w1, out):
    far_high, far_low = split(mm(h, edge_w1[:L]))
    near_high, near_low = split(mm(h, edge_w1[L : 2 * L]))
    table = jnp.concatenate([far_high, far_low, near_high, near_low], axis=0)
    for lo in range(0, fw.shape[0], CHUNK):
        out[lo : lo + CHUNK] = mm(tos[lo : lo + CHUNK], table) + fw[lo : lo + CHUNK]


def forward_kernel(
    p0, p1, p2, p3, q0, q1, q2, q3, pre_part, th, st_sent, edge_w1, node_w1, mix, node_w2, gain,
    s0, s1, s2, s3, pre_o, hidden_o,
):
    def keep(lo, pre):
        pre_o[lo : lo + CHUNK] = pre
        part = (pre * sigmoid(pre)).astype(BF16)
        hidden_o[lo : lo + CHUNK] = part
        return part

    hidden = edge_hidden([p0[...], p1[...], p2[...], p3[...]], th, pre_part, edge_w1, keep)
    h = jnp.concatenate([q0[...], q1[...], q2[...], q3[...]], axis=0)
    normed = node_body(h, mm(st_sent[...], hidden), node_w1, mix, node_w2)[2]
    sent = (h.astype(F32) + normed * gain[...]).astype(BF16)
    for i, out in enumerate((s0, s1, s2, s3)):
        out[...] = sent[i * HALO : (i + 1) * HALO]


def own_kernel(
    h_ref, pre, hidden, st, tos, fw, edge_w1, node_w1, mix, node_w2, gain,
    h_out, pre_part_o, edge_slope_o, hidden_sum_o, node_slope_o, hidden_node_o, normed_o, inv_dev_o,
):
    h = h_ref[...]
    hidden_sum = mm(st[...], hidden[...])
    node_slope, hidden_node, normed, inv_dev = node_body(h, hidden_sum, node_w1, mix, node_w2)
    nxt = (h.astype(F32) + normed * gain[...]).astype(BF16)
    h_out[...] = nxt
    own_pre(nxt, tos, fw, edge_w1, pre_part_o)
    edge_slope_o[...] = edge_slopes(pre[...])[1]
    hidden_sum_o[...] = hidden_sum
    node_slope_o[...] = node_slope
    hidden_node_o[...] = hidden_node
    normed_o[...] = normed
    inv_dev_o[...] = jnp.broadcast_to(inv_dev, inv_dev_o.shape)


def backward_body(
    up, parts, gain, ss, ttst, w1t, back, n2t, sends, gpe_o, qr_o, gpn_o, gu_o, gain_o
):
    edge_slope, node_slope, normed, inv_dev = parts
    gain_o[...] = jnp.sum(up * normed, axis=0, keepdims=True)
    scaled = up * gain
    gu = inv_dev * (
        scaled
        - jnp.mean(scaled, axis=-1, keepdims=True)
        - normed * jnp.mean(scaled * normed, axis=-1, keepdims=True)
    )
    gu = gu.astype(BF16)
    gpn = (mm(gu, n2t[...]) * node_slope).astype(BF16)
    gu_o[...] = gu
    gpn_o[...] = gpn
    gh = mm(gpn, back[:, 2 * L : 3 * L]) + mm(gpn, back[:, 3 * L :])
    high, low = split(gh)
    pair = jnp.concatenate([high, low], axis=0)
    gpe = []
    for lo in range(0, edge_slope.shape[0], CHUNK):
        part = (mm(ss[lo : lo + CHUNK], pair) * edge_slope[lo : lo + CHUNK]).astype(BF16)
        gpe_o[lo : lo + CHUNK] = part
        gpe.append(part)
    qr = mm(ttst[...], jnp.concatenate(gpe, axis=0))
    if sends:
        halo_grads(qr, w1t, sends)
    qr_o[...] = qr


def halo_grads(qr, w1t, sends):
    q_high, q_low = split(qr[OWN : 2 * OWN])
    far = w1t[:, :L]
    ge = mm(q_high, far) + mm(q_low, far)
    for i, out in enumerate(sends):
        out[...] = ge[i * HALO : (i + 1) * HALO].astype(BF16)


def rest_kernel(up, qr, gpn, w1t, back, own_out, *sends):
    if sends:
        halo_grads(qr, w1t, sends)
    q_high, q_low = split(qr[:OWN])
    r_high, r_low = split(qr[2 * OWN :])
    far, near = w1t[:, :L], w1t[:, L : 2 * L]
    own_out[...] = (
        up[...] + mm(gpn[...], back[:, :L]) + mm(q_high, far) + mm(q_low, far) + mm(r_high, near) + mm(r_low, near)
    )


def landed(own, spread, p0, p1, p2, p3):
    parts = jnp.concatenate([p0[...], p1[...], p2[...], p3[...]], axis=0)
    return own[...] + mm(spread[...], parts)


def turn_kernel(
    h_ref, p0, p1, p2, p3, pre_part, th, st, edge_w1, node_w1, mix, node_w2, gain, cot, ss, ttst, w1t, back, n2t,
    g0, g1, g2, g3, gpe_o, qr_o, gpn_o, gu_o, gain_o, hidden_sum_o, hidden_node_o, edge_slope,
):
    def keep(lo, pre):
        silu, slope = edge_slopes(pre)
        edge_slope[lo : lo + CHUNK] = slope
        return silu.astype(BF16)

    hidden = edge_hidden([p0[...], p1[...], p2[...], p3[...]], th, pre_part, edge_w1, keep)
    hidden_sum = mm(st[...], hidden)
    node_slope, hidden_node, normed, inv_dev = node_body(h_ref[...], hidden_sum, node_w1, mix, node_w2)
    hidden_sum_o[...] = hidden_sum
    hidden_node_o[...] = hidden_node
    backward_body(
        cot[...], (edge_slope, node_slope, normed, inv_dev), gain[...], ss, ttst, w1t, back, n2t,
        (g0, g1, g2, g3), gpe_o, qr_o, gpn_o, gu_o, gain_o,
    )


def backward_kernel(
    own, p0, p1, p2, p3, spread, edge_slope, node_slope, normed, inv_dev, gain, ss, ttst, w1t, back, n2t,
    gpe_o, qr_o, gpn_o, gu_o, gain_o, up_o, *sends,
):
    up = landed(own, spread, p0, p1, p2, p3)
    up_o[...] = up
    backward_body(
        up, (edge_slope, node_slope[...], normed[...], inv_dev[:, :1]), gain[...], ss, ttst, w1t, back, n2t,
        sends, gpe_o, qr_o, gpn_o, gu_o, gain_o,
    )


def weight_args(refs):
    h_ref, p0, p1, p2, p3, feats, edge_w2, hidden_sum, hidden_node, back, gpe, qr, gpn, gu = refs
    gm = mm(gpn[...], back[:, L : 2 * L]).astype(BF16)
    h = h_ref[...]
    extended = jnp.concatenate([h, p0[...], p1[...], p2[...], p3[...]], axis=0)
    qr_high, qr_low = split(qr[...])
    h_high, h_low = split(hidden_sum[...])
    summed = (mm(h_high, edge_w2[...]) + mm(h_low, edge_w2[...])).astype(BF16)
    return (
        mm_t(extended, qr_high[: 2 * OWN]) + mm_t(extended, qr_low[: 2 * OWN]),
        mm_t(h, qr_high[2 * OWN :]) + mm_t(h, qr_low[2 * OWN :]),
        mm_t(feats[...], gpe[...]),
        mm_t(h_high, gm) + mm_t(h_low, gm),
        mm_t(h, gpn[...]),
        mm_t(summed, gpn[...]),
        mm_t(hidden_node[...], gu[...]),
    )


def weight_first_kernel(*refs):
    w1t, gain_in, acc, edge_acc, gain_acc = refs[14:]
    for i, term in enumerate(weight_args(refs[:14])):
        acc[i] = term
    edge_acc[...] = mm(refs[10][...], w1t[:, 2 * L :])
    gain_acc[...] = gain_in[...]


def weight_kernel(*refs):
    w1t, gain_in, acc_in, edge_in, gain_acc_in, acc, edge_acc, gain_acc = refs[14:]
    for i, term in enumerate(weight_args(refs[:14])):
        acc[i] = acc_in[i] + term
    edge_acc[...] = edge_in[...] + mm(refs[10][...], w1t[:, 2 * L :])
    gain_acc[...] = gain_acc_in[...] + gain_in[...]


def weight_last_kernel(*refs):
    gain_in, acc_in, gain_acc_in, out = refs[14:]
    core = lax.axis_index("c")
    terms = weight_args(refs[:14])
    for i, term in enumerate(terms):
        out[(i // 4) ^ core, (i % 4) * L : (i % 4 + 1) * L, :] = (acc_in[i] + term).astype(BF16)
    row = lax.broadcasted_iota(jnp.int32, (L, L), 0)
    gain = gain_acc_in[...] + gain_in[...]
    out[1 ^ core, 3 * L :, :] = jnp.where(row == 0, gain, 0.0).astype(BF16)


def edge_last_kernel(gpe, w1t, edge_in, out):
    out[...] = edge_in[...] + mm(gpe[...], w1t[:, 2 * L :])


def node_last_kernel(own, p0, p1, p2, p3, spread, out):
    out[...] = landed(own, spread, p0, p1, p2, p3)


def finish_kernel(factor, mine, half_ref, *refs):
    edge_in, edge_out, node_in, node_out, gain, buf, row, sems = refs[-8:]
    core = lax.axis_index("c")
    which = core if mine else 1 - core
    targets = (
        (edge_in.at[:L], edge_in.at[L : 2 * L], edge_in.at[2 * L :], edge_out),
        (node_in.at[:L], node_in.at[L :], node_out, gain),
    )

    def copies(half, i):
        source = row if half == 1 and i == 3 else buf.at[i * L : (i + 1) * L]
        return pltpu.make_async_copy(source, targets[half][i], sems.at[i])

    for i in range(4):
        block = half_ref[i * L : (i + 1) * L].astype(F32) * factor
        buf[i * L : (i + 1) * L] = block
        if i == 3:
            row[...] = block[0]
        for half in range(2):
            pl.when(which == half)(lambda half=half, i=i: copies(half, i).start())
    for half in range(2):
        for i in range(4):
            pl.when(which == half)(lambda half=half, i=i: copies(half, i).wait())


def finish(factor, mine, half, *parts):
    outs = [((3 * L, L), F32), ((L, L), F32), ((2 * L, L), F32), ((L, L), F32), ((L,), F32)]
    hbm = pl.BlockSpec(memory_space=pltpu.HBM)
    return pl.pallas_call(
        functools.partial(finish_kernel, factor, mine),
        out_shape=[jax.ShapeDtypeStruct(s, d) for s, d in outs],
        in_specs=[pl.BlockSpec(memory_space=pltpu.VMEM)] + [hbm] * len(parts),
        out_specs=[hbm] * 5,
        input_output_aliases={i + 1: i for i in range(len(parts))},
        scratch_shapes=[pltpu.VMEM((4 * L, L), F32), pltpu.VMEM((L,), F32), pltpu.SemaphoreType.DMA((4,))],
        compiler_params=pltpu.CompilerParams(vmem_limit_bytes=32 * 1024 * 1024),
    )(half, *parts)


def even_pairs(size):
    return [(i, i ^ 1) for i in range(size)]


def odd_pairs(size):
    up = [((i + 1) % size, (i + 2) % size) for i in range(0, size, 2)]
    return up + [(b, a) for a, b in up]


def exchange(parts):
    slabs = lax.axis_size(SLAB)
    regions = lax.axis_size(REGION)
    return [
        lax.ppermute(parts[0], REGION, odd_pairs(regions)),
        lax.ppermute(parts[1], REGION, even_pairs(regions)),
        lax.ppermute(parts[2], SLAB, odd_pairs(slabs)),
        lax.ppermute(parts[3], SLAB, even_pairs(slabs)),
    ]


def reduce_all(payload, late):
    keep = payload[0].astype(F32)
    got = lax.ppermute(payload[1], "c", [(0, 1), (1, 0)])
    part = (keep + got.astype(F32)).astype(BF16).reshape(CHUNKS, CHUNK_ROWS, L)
    part = lax.all_to_all(part, PLANE, 0, 0, tiled=True)
    part = jnp.sum(part.astype(F32), axis=0).astype(BF16)
    deep = lax.axis_size("z")
    part = lax.all_to_all(jnp.broadcast_to(part[None], (deep,) + part.shape), "z", 0, 0, tiled=True)
    part = jnp.sum(part.astype(F32), axis=0).astype(BF16)
    part, *late = lax.optimization_barrier((part, *late))
    part = jnp.broadcast_to(part[None], (CHUNKS,) + part.shape)
    mine = lax.all_to_all(part, PLANE, 0, 0, tiled=True).reshape(CHUNKS * CHUNK_ROWS, L)
    other = lax.ppermute(mine, "c", [(0, 1), (1, 0)])
    return mine, other, late


def local(
    nodes, feats, cotangent, edge_w1, edge_w2, node_w1, node_w2, ln_gain, senders, receivers, send_rows, edge_count
):
    edges = feats.shape[0]
    halo_outs = [((HALO, L), BF16)] * 4
    *sends, spread = call(
        first_kernel, halo_outs + [((OWN, 4 * HALO), BF16)], nodes, send_rows, space=pltpu.HBM,
        scratch_shapes=[pltpu.VMEM((OWN, L), BF16), pltpu.VMEM((4, HALO), jnp.int32), pltpu.SemaphoreType.DMA((2,))],
    )
    tos, th, ss, ttst, st, st_sent, pre_part, fw, w1t, back_w, n2t, mix, gain, edge_w1, feats, node_w1, edge_w2, node_w2, cotangent, nodes = call(
        prep_kernel,
        [
            ((edges, 4 * OWN), BF16), ((edges, 2 * OWN), BF16), ((edges, 2 * OWN), BF16), ((3 * OWN, edges), BF16),
            ((OWN, edges), BF16), ((OWN, edges), BF16), ((edges, L), F32),
            ((edges, L), F32), ((L, 3 * L), BF16), ((L, 4 * L), BF16), ((L, L), BF16), ((L, 2 * L), BF16),
            ((1, L), F32), ((3 * L, L), BF16), ((edges, L), BF16), ((2 * L, L), BF16), ((L, L), BF16), ((L, L), BF16),
            ((OWN, L), F32), ((OWN, L), BF16),
        ],
        edge_count, senders, receivers, ln_gain, edge_w1, feats, node_w1, edge_w2, node_w2, cotangent, nodes, spread,
        space=pltpu.HBM,
        free=(0, 11),
        scratch_shapes=[
            pltpu.VMEM((OWN, 4 * HALO), BF16), pltpu.SMEM((1, 1), jnp.int32),
            pltpu.VMEM((edges,), jnp.int32), pltpu.VMEM((edges,), jnp.int32),
            pltpu.VMEM((L,), F32), pltpu.SemaphoreType.DMA((12,)),
        ],
    )
    h = nodes
    saved = []
    for _ in range(STEPS - 1):
        halo = exchange(sends)
        *sends, pre, hidden = call(
            forward_kernel,
            halo_outs + [((edges, L), F32), ((edges, L), BF16)],
            *halo, *sends, pre_part, th, st_sent, edge_w1, node_w1, mix, node_w2, gain,
        )
        nxt, pre_part, *rest = call(
            own_kernel,
            [
                ((OWN, L), BF16), ((edges, L), F32), ((edges, L), F32), ((OWN, L), F32), ((OWN, L), F32), ((OWN, L), BF16),
                ((OWN, L), F32), ((OWN, 128), F32),
            ],
            h, pre, hidden, st, tos, fw, edge_w1, node_w1, mix, node_w2, gain,
        )
        saved.append((h, halo, rest))
        h = nxt
    halo = exchange(sends)
    back_outs = [
        ((edges, L), BF16), ((3 * OWN, L), F32), ((OWN, L), BF16), ((OWN, L), BF16), ((1, L), F32),
    ]
    g0, g1, g2, g3, *terms, gain_term, hidden_sum, hidden_node = call(
        turn_kernel,
        halo_outs + back_outs + [((OWN, L), F32), ((OWN, L), BF16)],
        h, *halo, pre_part, th, st, edge_w1, node_w1, mix, node_w2, gain, cotangent, ss, ttst, w1t, back_w, n2t,
        scratch_shapes=[pltpu.VMEM((edges, L), F32)],
    )
    back = exchange([g0, g1, g2, g3])
    own_out = [((OWN, L), F32)]
    (own,) = call(rest_kernel, own_out, cotangent, terms[1], terms[2], w1t, back_w)
    acc_outs = [((7, L, L), F32), ((edges, L), F32), ((1, L), F32)]
    totals = call(
        weight_first_kernel, acc_outs, h, *halo, feats, edge_w2, hidden_sum, hidden_node, back_w, *terms, w1t, gain_term
    )
    for layer in reversed(range(STEPS - 1)):
        h, halo, (edge_slope, hidden_sum, node_slope, hidden_node, normed, inv_dev) = saved[layer]
        gpe, qr, gpn, gu, gain_term, up, *sends = call(
            backward_kernel, back_outs + own_out + (halo_outs if layer > 0 else []),
            own, *back, spread, edge_slope, node_slope, normed, inv_dev, gain, ss, ttst, w1t, back_w, n2t,
        )
        terms = (gpe, qr, gpn, gu)
        rest_outs = own_out if layer > 0 else own_out + halo_outs
        own, *late = call(rest_kernel, rest_outs, up, terms[1], terms[2], w1t, back_w)
        back = exchange(sends + late)
        shared = (h, *halo, feats, edge_w2, hidden_sum, hidden_node, back_w, *terms)
        if layer > 0:
            totals = call(weight_kernel, acc_outs, *shared, w1t, gain_term, *totals)
    (payload,) = call(
        weight_last_kernel, [((2, 4 * L, L), BF16)], *shared, gain_term, totals[0], totals[2]
    )
    (edge_grad,) = call(edge_last_kernel, [((edges, L), F32)], terms[0], w1t, totals[1])
    (node_grad,) = call(node_last_kernel, [((OWN, L), F32)], own, *back, spread)
    mine, other, (node_grad, edge_grad) = reduce_all(payload, (node_grad, edge_grad))
    devices = lax.axis_size(REGION) * lax.axis_size(SLAB)
    factor = float(OWN * devices) ** (-0.5)

    parts = finish(factor, True, mine)
    edge_in, edge_out, node_in, node_out, gain_grad = finish(factor, False, other, *parts)
    return node_grad, edge_grad, edge_in, edge_out, node_in, node_out, gain_grad


def solution(mesh):
    fine = Mesh(mesh.devices.reshape(4, 2, 8, 2, 2), AXES)
    split_rows = P(AXES, None)
    placed = (
        split_rows, split_rows, split_rows, P(), P(), P(), P(), P(), P(AXES), P(AXES), split_rows, P(REGION, SLAB),
    )
    return jax.shard_map(
        local,
        mesh=fine,
        in_specs=placed,
        out_specs=(split_rows, split_rows, P(), P(), P(), P(), P()),
        check_vma=False,
    )
```

```python
import functools

import jax
import jax.numpy as jnp
from jax import lax
from jax.experimental import pallas as pl
from jax.experimental.pallas import tpu as pltpu
from jax.sharding import Mesh
from jax.sharding import PartitionSpec as P

STEPS = 4
EPS = 1e-05
L = 256
OWN = 128
HALO = 32
BF16 = jnp.bfloat16
F32 = jnp.float32
AXES = ("x", "yh", "z", "yl", "c")
REGION = ("x", "yh")
SLAB = ("z", "yl", "c")
PLANE = ("yl", "yh", "x")
CHUNK = 128
EDGE_CHUNK = 640
CHUNKS = 16
CHUNK_ROWS = 64


def mm(a, b):
    return jnp.dot(a, b, preferred_element_type=F32)


def mm_t(a, b):
    return lax.dot_general(a, b, (((0,), (0,)), ((), ())), preferred_element_type=F32)


def split(v):
    high = v.astype(BF16)
    low = (v - high.astype(F32)).astype(BF16)
    return high, low


def mm_split(v, w):
    high, low = split(v)
    return mm(high, w) + mm(low, w)


def sigmoid(v):
    return 0.5 * jnp.tanh(0.5 * v) + 0.5


def call(kernel, outs, *args, space=pltpu.VMEM, free=(), **kw):
    specs = [pl.BlockSpec(memory_space=pl.ANY if i in free else space) for i in range(len(args))]
    if space is pltpu.HBM:
        args = [a if i in free else pltpu.with_memory_space_constraint(a, space) for i, a in enumerate(args)]
    return pl.pallas_call(
        kernel,
        out_shape=[jax.ShapeDtypeStruct(s, d) for s, d in outs],
        in_specs=specs,
        out_specs=[pl.BlockSpec(memory_space=pltpu.VMEM)] * len(outs),
        compiler_params=pltpu.CompilerParams(vmem_limit_bytes=32 * 1024 * 1024),
        **kw,
    )(*args)


def slot_lists(lists):
    slab_odd = lax.axis_index("c")
    region_odd = lax.axis_index("yh")
    a, b, c, d = (lists[i : i + 1, :] for i in range(4))
    return (
        jnp.where(region_odd == 1, d, c),
        jnp.where(region_odd == 1, c, d),
        jnp.where(slab_odd == 1, b, a),
        jnp.where(slab_odd == 1, a, b),
    )


def first_kernel(nodes, lists, s0, s1, s2, s3, spread, h, rows, sems):
    copies = [pltpu.make_async_copy(nodes, h, sems.at[0]), pltpu.make_async_copy(lists, rows, sems.at[1])]
    for copy in copies:
        copy.start()
    copies[1].wait()
    row = lax.broadcasted_iota(jnp.int32, (OWN, HALO), 0)
    hots = [(row == idx).astype(F32).astype(BF16) for idx in slot_lists(rows[...])]
    copies[0].wait()
    for i, (hot, out) in enumerate(zip(hots, (s0, s1, s2, s3))):
        spread[:, i * HALO : (i + 1) * HALO] = hot
        out[...] = mm_t(hot, h[...]).astype(BF16)


def prep_kernel(
    count_in, send_in, recv_in, gain_in, w1_in, feats_in, n1_in, w2_in, n2_in, cot_in, nodes_in, spread_in,
    tos_out, th_out, ss_out, ttst_out, st_out, st_sent_out, pre_out, fw_out, w1t_out, back_out, n2t_out, mix_out,
    gain_out, w1, feats, n1, w2, n2, cot, nodes,
    spread, count, send_idx, recv_idx, gain, sems,
):
    pairs = (
        (w1_in, w1), (feats_in, feats), (count_in, count), (spread_in, spread), (send_in, send_idx), (recv_in, recv_idx),
        (n1_in, n1), (w2_in, w2), (n2_in, n2), (nodes_in, nodes), (gain_in, gain), (cot_in, cot),
    )
    copies = [pltpu.make_async_copy(a, b, sems.at[i]) for i, (a, b) in enumerate(pairs)]
    for copy in copies:
        copy.start()
    for copy in copies:
        copy.wait()
    edges = feats.shape[0]
    lane = lax.broadcasted_iota(jnp.int32, (1, edges), 1)
    live = lane < count[0, 0]
    snd = send_idx[...].reshape(1, edges)
    off = snd - OWN
    slab_swap = jnp.where(lax.axis_index("c") == 1, 3 * HALO, 2 * HALO)
    region_swap = jnp.where(lax.axis_index("yh") == 1, 3 * HALO, 2 * HALO)
    flip = jnp.where(off < 2 * HALO, slab_swap, region_swap)
    snd = jnp.where(off >= 0, OWN + (off ^ flip), snd)
    snd = jnp.where(live, snd, -1)
    rcv = jnp.where(live, recv_idx[...].reshape(1, edges), -1)
    tt = (lax.broadcasted_iota(jnp.int32, (2 * OWN, edges), 0) == snd).astype(F32)
    st = (lax.broadcasted_iota(jnp.int32, (OWN, edges), 0) == rcv).astype(F32)
    spread_t = spread[...].T
    tt16 = tt.astype(BF16)
    st16 = st.astype(BF16)
    t16 = tt.T.astype(BF16)
    s16 = st.T.astype(BF16)
    ttst_out[: 2 * OWN] = tt16
    ttst_out[2 * OWN :] = st16
    st_out[...] = st16
    st_sent_out[...] = mm(spread_t, st16).astype(BF16)
    for i in range(2):
        tos_out[:, i * OWN : (i + 1) * OWN] = t16[:, :OWN]
        th_out[:, i * OWN : (i + 1) * OWN] = t16[:, OWN:]
        tos_out[:, (2 + i) * OWN : (3 + i) * OWN] = s16
        ss_out[:, i * OWN : (i + 1) * OWN] = s16
    fw_out[...] = mm(feats[...], w1[2 * L :])
    own_pre(nodes[...], tos_out, fw_out, w1, pre_out)
    w1t_out[...] = w1[...].T
    n2t_out[...] = n2[...].T
    mix_high, mix_low = split(mm(w2[...], n1[L:]))
    mix_out[:, :L] = mix_high
    mix_out[:, L:] = mix_low
    back_out[:, : 2 * L] = n1[...].T
    back_out[:, 2 * L : 3 * L] = mix_high.T
    back_out[:, 3 * L :] = mix_low.T
    gain_out[...] = gain[...].reshape(1, L)


def edge_hidden(halo, th, pre_part, edge_w1, keep):
    high, low = split(mm(jnp.concatenate(halo, axis=0), edge_w1[:L]))
    table = jnp.concatenate([high, low], axis=0)
    hidden = []
    for lo in range(0, pre_part.shape[0], EDGE_CHUNK):
        pre = mm(th[lo : lo + EDGE_CHUNK], table) + pre_part[lo : lo + EDGE_CHUNK]
        hidden.append(keep(lo, pre))
    return jnp.concatenate(hidden, axis=0)


def edge_slopes(pre):
    sig = sigmoid(pre)
    silu = pre * sig
    return silu, sig + silu * (1.0 - sig)


def node_body(h, hidden_sum, node_w1, mix, node_w2):
    high, low = split(hidden_sum)
    pre_node = mm(h, node_w1[:L]) + mm(high, mix[:, :L]) + mm(high, mix[:, L:]) + mm(low, mix[:, :L])
    silu_n, node_slope = edge_slopes(pre_node)
    hidden_node = silu_n.astype(BF16)
    update = mm(hidden_node, node_w2[...])
    centre = update - jnp.mean(update, axis=-1, keepdims=True)
    inv_dev = lax.rsqrt(jnp.mean(centre * centre, axis=-1, keepdims=True) + EPS)
    return node_slope, hidden_node, centre * inv_dev, inv_dev


def own_pre(h, tos, fw, edge_w1, out):
    far_high, far_low = split(mm(h, edge_w1[:L]))
    near_high, near_low = split(mm(h, edge_w1[L : 2 * L]))
    table = jnp.concatenate([far_high, far_low, near_high, near_low], axis=0)
    for lo in range(0, fw.shape[0], CHUNK):
        out[lo : lo + CHUNK] = mm(tos[lo : lo + CHUNK], table) + fw[lo : lo + CHUNK]


def forward_kernel(
    p0, p1, p2, p3, q0, q1, q2, q3, pre_part, th, st_sent, edge_w1, node_w1, mix, node_w2, gain,
    s0, s1, s2, s3, pre_o, hidden_o,
):
    def keep(lo, pre):
        pre_o[lo : lo + EDGE_CHUNK] = pre
        part = (pre * sigmoid(pre)).astype(BF16)
        hidden_o[lo : lo + EDGE_CHUNK] = part
        return part

    hidden = edge_hidden([p0[...], p1[...], p2[...], p3[...]], th, pre_part, edge_w1, keep)
    h = jnp.concatenate([q0[...], q1[...], q2[...], q3[...]], axis=0)
    normed = node_body(h, mm(st_sent[...], hidden), node_w1, mix, node_w2)[2]
    sent = (h.astype(F32) + normed * gain[...]).astype(BF16)
    for i, out in enumerate((s0, s1, s2, s3)):
        out[...] = sent[i * HALO : (i + 1) * HALO]


def own_kernel(
    h_ref, pre, hidden, st, tos, fw, edge_w1, node_w1, mix, node_w2, gain,
    h_out, pre_part_o, edge_slope_o, hidden_sum_o, node_slope_o, hidden_node_o, normed_o, inv_dev_o,
):
    h = h_ref[...]
    hidden_sum = mm(st[...], hidden[...])
    node_slope, hidden_node, normed, inv_dev = node_body(h, hidden_sum, node_w1, mix, node_w2)
    nxt = (h.astype(F32) + normed * gain[...]).astype(BF16)
    h_out[...] = nxt
    own_pre(nxt, tos, fw, edge_w1, pre_part_o)
    edge_slope_o[...] = edge_slopes(pre[...])[1]
    hidden_sum_o[...] = hidden_sum
    node_slope_o[...] = node_slope
    hidden_node_o[...] = hidden_node
    normed_o[...] = normed
    inv_dev_o[...] = jnp.broadcast_to(inv_dev, inv_dev_o.shape)


def backward_body(
    up, parts, gain, ss, ttst, w1t, back, n2t, sends, gpe_o, qr_o, gpn_o, gu_o, gain_o
):
    edge_slope, node_slope, normed, inv_dev = parts
    gain_o[...] = jnp.sum(up * normed, axis=0, keepdims=True)
    scaled = up * gain
    gu = inv_dev * (
        scaled
        - jnp.mean(scaled, axis=-1, keepdims=True)
        - normed * jnp.mean(scaled * normed, axis=-1, keepdims=True)
    )
    gu = gu.astype(BF16)
    gpn = (mm(gu, n2t[...]) * node_slope).astype(BF16)
    gu_o[...] = gu
    gpn_o[...] = gpn
    gh = mm(gpn, back[:, 2 * L : 3 * L]) + mm(gpn, back[:, 3 * L :])
    high, low = split(gh)
    pair = jnp.concatenate([high, low], axis=0)
    gpe = []
    for lo in range(0, edge_slope.shape[0], CHUNK):
        part = (mm(ss[lo : lo + CHUNK], pair) * edge_slope[lo : lo + CHUNK]).astype(BF16)
        gpe_o[lo : lo + CHUNK] = part
        gpe.append(part)
    qr = mm(ttst[...], jnp.concatenate(gpe, axis=0))
    if sends:
        halo_grads(qr, w1t, sends)
    qr_o[...] = qr


def halo_grads(qr, w1t, sends):
    q_high, q_low = split(qr[OWN : 2 * OWN])
    far = w1t[:, :L]
    ge = mm(q_high, far) + mm(q_low, far)
    for i, out in enumerate(sends):
        out[...] = ge[i * HALO : (i + 1) * HALO].astype(BF16)


def rest_kernel(up, qr, gpn, w1t, back, own_out, *sends):
    if sends:
        halo_grads(qr, w1t, sends)
    q_high, q_low = split(qr[:OWN])
    r_high, r_low = split(qr[2 * OWN :])
    far, near = w1t[:, :L], w1t[:, L : 2 * L]
    own_out[...] = (
        up[...] + mm(gpn[...], back[:, :L]) + mm(q_high, far) + mm(q_low, far) + mm(r_high, near) + mm(r_low, near)
    )


def landed(own, spread, p0, p1, p2, p3):
    parts = jnp.concatenate([p0[...], p1[...], p2[...], p3[...]], axis=0)
    return own[...] + mm(spread[...], parts)


def turn_kernel(
    h_ref, p0, p1, p2, p3, pre_part, th, st, edge_w1, node_w1, mix, node_w2, gain, cot, ss, ttst, w1t, back, n2t,
    g0, g1, g2, g3, gpe_o, qr_o, gpn_o, gu_o, gain_o, hidden_sum_o, hidden_node_o, edge_slope,
):
    def keep(lo, pre):
        silu, slope = edge_slopes(pre)
        edge_slope[lo : lo + EDGE_CHUNK] = slope
        return silu.astype(BF16)

    hidden = edge_hidden([p0[...], p1[...], p2[...], p3[...]], th, pre_part, edge_w1, keep)
    hidden_sum = mm(st[...], hidden)
    node_slope, hidden_node, normed, inv_dev = node_body(h_ref[...], hidden_sum, node_w1, mix, node_w2)
    hidden_sum_o[...] = hidden_sum
    hidden_node_o[...] = hidden_node
    backward_body(
        cot[...], (edge_slope, node_slope, normed, inv_dev), gain[...], ss, ttst, w1t, back, n2t,
        (g0, g1, g2, g3), gpe_o, qr_o, gpn_o, gu_o, gain_o,
    )


def backward_kernel(
    own, p0, p1, p2, p3, spread, edge_slope, node_slope, normed, inv_dev, gain, ss, ttst, w1t, back, n2t,
    gpe_o, qr_o, gpn_o, gu_o, gain_o, up_o, *sends,
):
    up = landed(own, spread, p0, p1, p2, p3)
    up_o[...] = up
    backward_body(
        up, (edge_slope, node_slope[...], normed[...], inv_dev[:, :1]), gain[...], ss, ttst, w1t, back, n2t,
        sends, gpe_o, qr_o, gpn_o, gu_o, gain_o,
    )


def weight_args(refs):
    h_ref, p0, p1, p2, p3, feats, edge_w2, hidden_sum, hidden_node, back, gpe, qr, gpn, gu = refs
    gm = mm(gpn[...], back[:, L : 2 * L]).astype(BF16)
    h = h_ref[...]
    extended = jnp.concatenate([h, p0[...], p1[...], p2[...], p3[...]], axis=0)
    qr_high, qr_low = split(qr[...])
    h_high, h_low = split(hidden_sum[...])
    summed = (mm(h_high, edge_w2[...]) + mm(h_low, edge_w2[...])).astype(BF16)
    return (
        mm_t(extended, qr_high[: 2 * OWN]) + mm_t(extended, qr_low[: 2 * OWN]),
        mm_t(h, qr_high[2 * OWN :]) + mm_t(h, qr_low[2 * OWN :]),
        mm_t(feats[...], gpe[...]),
        mm_t(h_high, gm) + mm_t(h_low, gm),
        mm_t(h, gpn[...]),
        mm_t(summed, gpn[...]),
        mm_t(hidden_node[...], gu[...]),
    )


def weight_first_kernel(*refs):
    w1t, gain_in, acc, edge_acc, gain_acc = refs[14:]
    for i, term in enumerate(weight_args(refs[:14])):
        acc[i] = term
    edge_acc[...] = mm(refs[10][...], w1t[:, 2 * L :])
    gain_acc[...] = gain_in[...]


def weight_kernel(*refs):
    w1t, gain_in, acc_in, edge_in, gain_acc_in, acc, edge_acc, gain_acc = refs[14:]
    for i, term in enumerate(weight_args(refs[:14])):
        acc[i] = acc_in[i] + term
    edge_acc[...] = edge_in[...] + mm(refs[10][...], w1t[:, 2 * L :])
    gain_acc[...] = gain_acc_in[...] + gain_in[...]


def weight_last_kernel(*refs):
    gain_in, acc_in, gain_acc_in, out = refs[14:]
    core = lax.axis_index("c")
    terms = weight_args(refs[:14])
    for i, term in enumerate(terms):
        out[(i // 4) ^ core, (i % 4) * L : (i % 4 + 1) * L, :] = (acc_in[i] + term).astype(BF16)
    row = lax.broadcasted_iota(jnp.int32, (L, L), 0)
    gain = gain_acc_in[...] + gain_in[...]
    out[1 ^ core, 3 * L :, :] = jnp.where(row == 0, gain, 0.0).astype(BF16)


def edge_last_kernel(gpe, w1t, edge_in, out):
    out[...] = edge_in[...] + mm(gpe[...], w1t[:, 2 * L :])


def node_last_kernel(own, p0, p1, p2, p3, spread, out):
    out[...] = landed(own, spread, p0, p1, p2, p3)


def finish_kernel(factor, mine, half_ref, *refs):
    edge_in, edge_out, node_in, node_out, gain, buf, row, sems = refs[-8:]
    core = lax.axis_index("c")
    which = core if mine else 1 - core
    targets = (
        (edge_in.at[:L], edge_in.at[L : 2 * L], edge_in.at[2 * L :], edge_out),
        (node_in.at[:L], node_in.at[L :], node_out, gain),
    )

    def copies(half, i):
        source = row if half == 1 and i == 3 else buf.at[i * L : (i + 1) * L]
        return pltpu.make_async_copy(source, targets[half][i], sems.at[i])

    for i in range(4):
        block = half_ref[i * L : (i + 1) * L].astype(F32) * factor
        buf[i * L : (i + 1) * L] = block
        if i == 3:
            row[...] = block[0]
        for half in range(2):
            pl.when(which == half)(lambda half=half, i=i: copies(half, i).start())
    for half in range(2):
        for i in range(4):
            pl.when(which == half)(lambda half=half, i=i: copies(half, i).wait())


def finish(factor, mine, half, *parts):
    outs = [((3 * L, L), F32), ((L, L), F32), ((2 * L, L), F32), ((L, L), F32), ((L,), F32)]
    hbm = pl.BlockSpec(memory_space=pltpu.HBM)
    return pl.pallas_call(
        functools.partial(finish_kernel, factor, mine),
        out_shape=[jax.ShapeDtypeStruct(s, d) for s, d in outs],
        in_specs=[pl.BlockSpec(memory_space=pltpu.VMEM)] + [hbm] * len(parts),
        out_specs=[hbm] * 5,
        input_output_aliases={i + 1: i for i in range(len(parts))},
        scratch_shapes=[pltpu.VMEM((4 * L, L), F32), pltpu.VMEM((L,), F32), pltpu.SemaphoreType.DMA((4,))],
        compiler_params=pltpu.CompilerParams(vmem_limit_bytes=32 * 1024 * 1024),
    )(half, *parts)


def even_pairs(size):
    return [(i, i ^ 1) for i in range(size)]


def odd_pairs(size):
    up = [((i + 1) % size, (i + 2) % size) for i in range(0, size, 2)]
    return up + [(b, a) for a, b in up]


def exchange(parts):
    slabs = lax.axis_size(SLAB)
    regions = lax.axis_size(REGION)
    return [
        lax.ppermute(parts[0], REGION, odd_pairs(regions)),
        lax.ppermute(parts[1], REGION, even_pairs(regions)),
        lax.ppermute(parts[2], SLAB, odd_pairs(slabs)),
        lax.ppermute(parts[3], SLAB, even_pairs(slabs)),
    ]


def reduce_all(payload, late):
    keep = payload[0].astype(F32)
    got = lax.ppermute(payload[1], "c", [(0, 1), (1, 0)])
    part = (keep + got.astype(F32)).astype(BF16).reshape(CHUNKS, CHUNK_ROWS, L)
    part = lax.all_to_all(part, PLANE, 0, 0, tiled=True)
    part = jnp.sum(part.astype(F32), axis=0).astype(BF16)
    deep = lax.axis_size("z")
    part = lax.all_to_all(jnp.broadcast_to(part[None], (deep,) + part.shape), "z", 0, 0, tiled=True)
    part = jnp.sum(part.astype(F32), axis=0).astype(BF16)
    part, *late = lax.optimization_barrier((part, *late))
    part = jnp.broadcast_to(part[None], (CHUNKS,) + part.shape)
    mine = lax.all_to_all(part, PLANE, 0, 0, tiled=True).reshape(CHUNKS * CHUNK_ROWS, L)
    other = lax.ppermute(mine, "c", [(0, 1), (1, 0)])
    return mine, other, late


def local(
    nodes, feats, cotangent, edge_w1, edge_w2, node_w1, node_w2, ln_gain, senders, receivers, send_rows, edge_count
):
    edges = feats.shape[0]
    halo_outs = [((HALO, L), BF16)] * 4
    *sends, spread = call(
        first_kernel, halo_outs + [((OWN, 4 * HALO), BF16)], nodes, send_rows, space=pltpu.HBM,
        scratch_shapes=[pltpu.VMEM((OWN, L), BF16), pltpu.VMEM((4, HALO), jnp.int32), pltpu.SemaphoreType.DMA((2,))],
    )
    tos, th, ss, ttst, st, st_sent, pre_part, fw, w1t, back_w, n2t, mix, gain, edge_w1, feats, node_w1, edge_w2, node_w2, cotangent, nodes = call(
        prep_kernel,
        [
            ((edges, 4 * OWN), BF16), ((edges, 2 * OWN), BF16), ((edges, 2 * OWN), BF16), ((3 * OWN, edges), BF16),
            ((OWN, edges), BF16), ((OWN, edges), BF16), ((edges, L), F32),
            ((edges, L), F32), ((L, 3 * L), BF16), ((L, 4 * L), BF16), ((L, L), BF16), ((L, 2 * L), BF16),
            ((1, L), F32), ((3 * L, L), BF16), ((edges, L), BF16), ((2 * L, L), BF16), ((L, L), BF16), ((L, L), BF16),
            ((OWN, L), F32), ((OWN, L), BF16),
        ],
        edge_count, senders, receivers, ln_gain, edge_w1, feats, node_w1, edge_w2, node_w2, cotangent, nodes, spread,
        space=pltpu.HBM,
        free=(0, 11),
        scratch_shapes=[
            pltpu.VMEM((OWN, 4 * HALO), BF16), pltpu.SMEM((1, 1), jnp.int32),
            pltpu.VMEM((edges,), jnp.int32), pltpu.VMEM((edges,), jnp.int32),
            pltpu.VMEM((L,), F32), pltpu.SemaphoreType.DMA((12,)),
        ],
    )
    h = nodes
    saved = []
    for _ in range(STEPS - 1):
        halo = exchange(sends)
        *sends, pre, hidden = call(
            forward_kernel,
            halo_outs + [((edges, L), F32), ((edges, L), BF16)],
            *halo, *sends, pre_part, th, st_sent, edge_w1, node_w1, mix, node_w2, gain,
        )
        nxt, pre_part, *rest = call(
            own_kernel,
            [
                ((OWN, L), BF16), ((edges, L), F32), ((edges, L), F32), ((OWN, L), F32), ((OWN, L), F32), ((OWN, L), BF16),
                ((OWN, L), F32), ((OWN, 128), F32),
            ],
            h, pre, hidden, st, tos, fw, edge_w1, node_w1, mix, node_w2, gain,
        )
        saved.append((h, halo, rest))
        h = nxt
    halo = exchange(sends)
    back_outs = [
        ((edges, L), BF16), ((3 * OWN, L), F32), ((OWN, L), BF16), ((OWN, L), BF16), ((1, L), F32),
    ]
    g0, g1, g2, g3, *terms, gain_term, hidden_sum, hidden_node = call(
        turn_kernel,
        halo_outs + back_outs + [((OWN, L), F32), ((OWN, L), BF16)],
        h, *halo, pre_part, th, st, edge_w1, node_w1, mix, node_w2, gain, cotangent, ss, ttst, w1t, back_w, n2t,
        scratch_shapes=[pltpu.VMEM((edges, L), F32)],
    )
    back = exchange([g0, g1, g2, g3])
    own_out = [((OWN, L), F32)]
    (own,) = call(rest_kernel, own_out, cotangent, terms[1], terms[2], w1t, back_w)
    acc_outs = [((7, L, L), F32), ((edges, L), F32), ((1, L), F32)]
    totals = call(
        weight_first_kernel, acc_outs, h, *halo, feats, edge_w2, hidden_sum, hidden_node, back_w, *terms, w1t, gain_term
    )
    for layer in reversed(range(STEPS - 1)):
        h, halo, (edge_slope, hidden_sum, node_slope, hidden_node, normed, inv_dev) = saved[layer]
        gpe, qr, gpn, gu, gain_term, up, *sends = call(
            backward_kernel, back_outs + own_out + (halo_outs if layer > 0 else []),
            own, *back, spread, edge_slope, node_slope, normed, inv_dev, gain, ss, ttst, w1t, back_w, n2t,
        )
        terms = (gpe, qr, gpn, gu)
        rest_outs = own_out if layer > 0 else own_out + halo_outs
        own, *late = call(rest_kernel, rest_outs, up, terms[1], terms[2], w1t, back_w)
        back = exchange(sends + late)
        shared = (h, *halo, feats, edge_w2, hidden_sum, hidden_node, back_w, *terms)
        if layer > 0:
            totals = call(weight_kernel, acc_outs, *shared, w1t, gain_term, *totals)
    (payload,) = call(
        weight_last_kernel, [((2, 4 * L, L), BF16)], *shared, gain_term, totals[0], totals[2]
    )
    (edge_grad,) = call(edge_last_kernel, [((edges, L), F32)], terms[0], w1t, totals[1])
    (node_grad,) = call(node_last_kernel, [((OWN, L), F32)], own, *back, spread)
    mine, other, (node_grad, edge_grad) = reduce_all(payload, (node_grad, edge_grad))
    devices = lax.axis_size(REGION) * lax.axis_size(SLAB)
    factor = float(OWN * devices) ** (-0.5)

    parts = finish(factor, True, mine)
    edge_in, edge_out, node_in, node_out, gain_grad = finish(factor, False, other, *parts)
    return node_grad, edge_grad, edge_in, edge_out, node_in, node_out, gain_grad


def solution(mesh):
    fine = Mesh(mesh.devices.reshape(4, 2, 8, 2, 2), AXES)
    split_rows = P(AXES, None)
    placed = (
        split_rows, split_rows, split_rows, P(), P(), P(), P(), P(), P(AXES), P(AXES), split_rows, P(REGION, SLAB),
    )
    return jax.shard_map(
        local,
        mesh=fine,
        in_specs=placed,
        out_specs=(split_rows, split_rows, P(), P(), P(), P(), P()),
        check_vma=False,
    )
```

```python
import functools

import jax
import jax.numpy as jnp
from jax import lax
from jax.experimental import pallas as pl
from jax.experimental.pallas import tpu as pltpu
from jax.sharding import Mesh
from jax.sharding import PartitionSpec as P

STEPS = 4
EPS = 1e-05
L = 256
OWN = 128
HALO = 32
BF16 = jnp.bfloat16
F32 = jnp.float32
AXES = ("x", "yh", "z", "yl", "c")
REGION = ("x", "yh")
SLAB = ("z", "yl", "c")
PLANE = ("yl", "yh", "x")
CHUNK = 128
EDGE_CHUNK = 640
CHUNKS = 16
CHUNK_ROWS = 64


def mm(a, b):
    return jnp.dot(a, b, preferred_element_type=F32)


def mm_t(a, b):
    return lax.dot_general(a, b, (((0,), (0,)), ((), ())), preferred_element_type=F32)


def split(v):
    high = v.astype(BF16)
    low = (v - high.astype(F32)).astype(BF16)
    return high, low


def mm_split(v, w):
    high, low = split(v)
    return mm(high, w) + mm(low, w)


def sigmoid(v):
    return 0.5 * jnp.tanh(0.5 * v) + 0.5


def call(kernel, outs, *args, space=pltpu.VMEM, free=(), **kw):
    specs = [pl.BlockSpec(memory_space=pl.ANY if i in free else space) for i in range(len(args))]
    if space is pltpu.HBM:
        args = [a if i in free else pltpu.with_memory_space_constraint(a, space) for i, a in enumerate(args)]
    return pl.pallas_call(
        kernel,
        out_shape=[jax.ShapeDtypeStruct(s, d) for s, d in outs],
        in_specs=specs,
        out_specs=[pl.BlockSpec(memory_space=pltpu.VMEM)] * len(outs),
        compiler_params=pltpu.CompilerParams(vmem_limit_bytes=32 * 1024 * 1024),
        **kw,
    )(*args)


def slot_lists(lists):
    slab_odd = lax.axis_index("c")
    region_odd = lax.axis_index("yh")
    a, b, c, d = (lists[i : i + 1, :] for i in range(4))
    return (
        jnp.where(region_odd == 1, d, c),
        jnp.where(region_odd == 1, c, d),
        jnp.where(slab_odd == 1, b, a),
        jnp.where(slab_odd == 1, a, b),
    )


def first_kernel(nodes, lists, s0, s1, s2, s3, spread, h, rows, sems):
    copies = [pltpu.make_async_copy(nodes, h, sems.at[0]), pltpu.make_async_copy(lists, rows, sems.at[1])]
    for copy in copies:
        copy.start()
    copies[1].wait()
    row = lax.broadcasted_iota(jnp.int32, (OWN, HALO), 0)
    hots = [(row == idx).astype(F32).astype(BF16) for idx in slot_lists(rows[...])]
    copies[0].wait()
    for i, (hot, out) in enumerate(zip(hots, (s0, s1, s2, s3))):
        spread[:, i * HALO : (i + 1) * HALO] = hot
        out[...] = mm_t(hot, h[...]).astype(BF16)


def prep_kernel(
    count_in, send_in, recv_in, gain_in, w1_in, feats_in, n1_in, w2_in, n2_in, cot_in, nodes_in, spread_in,
    tos_out, th_out, ss_out, ttst_out, st_out, st_sent_out, pre_out, fw_out, w1t_out, back_out, n2t_out, mix_out,
    gain_out, w1, feats, n1, w2, n2, cot, nodes,
    spread, count, send_idx, recv_idx, gain, sems,
):
    pairs = (
        (w1_in, w1), (feats_in, feats), (count_in, count), (spread_in, spread), (send_in, send_idx), (recv_in, recv_idx),
        (n1_in, n1), (w2_in, w2), (n2_in, n2), (nodes_in, nodes), (gain_in, gain), (cot_in, cot),
    )
    copies = [pltpu.make_async_copy(a, b, sems.at[i]) for i, (a, b) in enumerate(pairs)]
    for copy in copies:
        copy.start()
    for copy in copies:
        copy.wait()
    edges = feats.shape[0]
    lane = lax.broadcasted_iota(jnp.int32, (1, edges), 1)
    live = lane < count[0, 0]
    snd = send_idx[...].reshape(1, edges)
    off = snd - OWN
    slab_swap = jnp.where(lax.axis_index("c") == 1, 3 * HALO, 2 * HALO)
    region_swap = jnp.where(lax.axis_index("yh") == 1, 3 * HALO, 2 * HALO)
    flip = jnp.where(off < 2 * HALO, slab_swap, region_swap)
    snd = jnp.where(off >= 0, OWN + (off ^ flip), snd)
    snd = jnp.where(live, snd, -1)
    rcv = jnp.where(live, recv_idx[...].reshape(1, edges), -1)
    tt = (lax.broadcasted_iota(jnp.int32, (2 * OWN, edges), 0) == snd).astype(F32)
    st = (lax.broadcasted_iota(jnp.int32, (OWN, edges), 0) == rcv).astype(F32)
    spread_t = spread[...].T
    tt16 = tt.astype(BF16)
    st16 = st.astype(BF16)
    t16 = tt.T.astype(BF16)
    s16 = st.T.astype(BF16)
    ttst_out[: 2 * OWN] = tt16
    ttst_out[2 * OWN :] = st16
    st_out[...] = st16
    st_sent_out[...] = mm(spread_t, st16).astype(BF16)
    for i in range(2):
        tos_out[:, i * OWN : (i + 1) * OWN] = t16[:, :OWN]
        th_out[:, i * OWN : (i + 1) * OWN] = t16[:, OWN:]
        tos_out[:, (2 + i) * OWN : (3 + i) * OWN] = s16
        ss_out[:, i * OWN : (i + 1) * OWN] = s16
    fw_out[...] = mm(feats[...], w1[2 * L :])
    own_pre(nodes[...], tos_out, fw_out, w1, pre_out)
    w1t_out[...] = w1[...].T
    n2t_out[...] = n2[...].T
    mix_high, mix_low = split(mm(w2[...], n1[L:]))
    mix_out[:, :L] = mix_high
    mix_out[:, L:] = mix_low
    back_out[:, : 2 * L] = n1[...].T
    back_out[:, 2 * L : 3 * L] = mix_high.T
    back_out[:, 3 * L :] = mix_low.T
    gain_out[...] = gain[...].reshape(1, L)


def edge_hidden(halo, th, pre_part, edge_w1, keep):
    high, low = split(mm(jnp.concatenate(halo, axis=0), edge_w1[:L]))
    table = jnp.concatenate([high, low], axis=0)
    hidden = []
    for lo in range(0, pre_part.shape[0], EDGE_CHUNK):
        pre = mm(th[lo : lo + EDGE_CHUNK], table) + pre_part[lo : lo + EDGE_CHUNK]
        hidden.append(keep(lo, pre))
    return jnp.concatenate(hidden, axis=0)


def edge_slopes(pre):
    sig = sigmoid(pre)
    silu = pre * sig
    return silu, sig + silu * (1.0 - sig)


def node_body(h, hidden_sum, node_w1, mix, node_w2):
    high, low = split(hidden_sum)
    pre_node = mm(h, node_w1[:L]) + mm(high, mix[:, :L]) + mm(high, mix[:, L:]) + mm(low, mix[:, :L])
    silu_n, node_slope = edge_slopes(pre_node)
    hidden_node = silu_n.astype(BF16)
    update = mm(hidden_node, node_w2[...])
    centre = update - jnp.mean(update, axis=-1, keepdims=True)
    inv_dev = lax.rsqrt(jnp.mean(centre * centre, axis=-1, keepdims=True) + EPS)
    return node_slope, hidden_node, centre * inv_dev, inv_dev


def own_pre(h, tos, fw, edge_w1, out):
    far_high, far_low = split(mm(h, edge_w1[:L]))
    near_high, near_low = split(mm(h, edge_w1[L : 2 * L]))
    table = jnp.concatenate([far_high, far_low, near_high, near_low], axis=0)
    for lo in range(0, fw.shape[0], CHUNK):
        out[lo : lo + CHUNK] = mm(tos[lo : lo + CHUNK], table) + fw[lo : lo + CHUNK]


def forward_kernel(
    p0, p1, p2, p3, q0, q1, q2, q3, pre_part, th, st_sent, edge_w1, node_w1, mix, node_w2, gain,
    s0, s1, s2, s3, pre_o, hidden_o,
):
    def keep(lo, pre):
        pre_o[lo : lo + EDGE_CHUNK] = pre
        part = (pre * sigmoid(pre)).astype(BF16)
        hidden_o[lo : lo + EDGE_CHUNK] = part
        return part

    hidden = edge_hidden([p0[...], p1[...], p2[...], p3[...]], th, pre_part, edge_w1, keep)
    h = jnp.concatenate([q0[...], q1[...], q2[...], q3[...]], axis=0)
    normed = node_body(h, mm(st_sent[...], hidden), node_w1, mix, node_w2)[2]
    sent = (h.astype(F32) + normed * gain[...]).astype(BF16)
    for i, out in enumerate((s0, s1, s2, s3)):
        out[...] = sent[i * HALO : (i + 1) * HALO]


def own_kernel(
    h_ref, pre, hidden, st, tos, fw, edge_w1, node_w1, mix, node_w2, gain,
    h_out, pre_part_o, edge_slope_o, hidden_sum_o, node_slope_o, hidden_node_o, normed_o, inv_dev_o,
):
    h = h_ref[...]
    hidden_sum = mm(st[...], hidden[...])
    node_slope, hidden_node, normed, inv_dev = node_body(h, hidden_sum, node_w1, mix, node_w2)
    nxt = (h.astype(F32) + normed * gain[...]).astype(BF16)
    h_out[...] = nxt
    own_pre(nxt, tos, fw, edge_w1, pre_part_o)
    edge_slope_o[...] = edge_slopes(pre[...])[1]
    hidden_sum_o[...] = hidden_sum
    node_slope_o[...] = node_slope
    hidden_node_o[...] = hidden_node
    normed_o[...] = normed
    inv_dev_o[...] = jnp.broadcast_to(inv_dev, inv_dev_o.shape)


def backward_body(
    up, parts, gain, ss, ttst, w1t, back, n2t, sends, gpe_o, qr_o, gpn_o, gu_o, gain_o
):
    edge_slope, node_slope, normed, inv_dev = parts
    gain_o[...] = jnp.sum(up * normed, axis=0, keepdims=True)
    scaled = up * gain
    gu = inv_dev * (
        scaled
        - jnp.mean(scaled, axis=-1, keepdims=True)
        - normed * jnp.mean(scaled * normed, axis=-1, keepdims=True)
    )
    gu = gu.astype(BF16)
    gpn = (mm(gu, n2t[...]) * node_slope).astype(BF16)
    gu_o[...] = gu
    gpn_o[...] = gpn
    gh = mm(gpn, back[:, 2 * L : 3 * L]) + mm(gpn, back[:, 3 * L :])
    high, low = split(gh)
    pair = jnp.concatenate([high, low], axis=0)
    gpe = []
    for lo in range(0, edge_slope.shape[0], CHUNK):
        part = (mm(ss[lo : lo + CHUNK], pair) * edge_slope[lo : lo + CHUNK]).astype(BF16)
        gpe_o[lo : lo + CHUNK] = part
        gpe.append(part)
    qr = mm(ttst[...], jnp.concatenate(gpe, axis=0))
    if sends:
        halo_grads(qr, w1t, sends)
    qr_o[...] = qr


def halo_grads(qr, w1t, sends):
    q_high, q_low = split(qr[OWN : 2 * OWN])
    far = w1t[:, :L]
    ge = mm(q_high, far) + mm(q_low, far)
    for i, out in enumerate(sends):
        out[...] = ge[i * HALO : (i + 1) * HALO].astype(BF16)


def rest_kernel(up, qr, gpn, w1t, back, own_out, *sends):
    if sends:
        halo_grads(qr, w1t, sends)
    q_high, q_low = split(qr[:OWN])
    r_high, r_low = split(qr[2 * OWN :])
    far, near = w1t[:, :L], w1t[:, L : 2 * L]
    own_out[...] = (
        up[...] + mm(gpn[...], back[:, :L]) + mm(q_high, far) + mm(q_low, far) + mm(r_high, near) + mm(r_low, near)
    )


def landed(own, spread, p0, p1, p2, p3):
    parts = jnp.concatenate([p0[...], p1[...], p2[...], p3[...]], axis=0)
    return own[...] + mm(spread[...], parts)


def turn_kernel(
    h_ref, p0, p1, p2, p3, pre_part, th, st, edge_w1, node_w1, mix, node_w2, gain, cot, ss, ttst, w1t, back, n2t,
    g0, g1, g2, g3, gpe_o, qr_o, gpn_o, gu_o, gain_o, hidden_sum_o, hidden_node_o, edge_slope,
):
    def keep(lo, pre):
        silu, slope = edge_slopes(pre)
        edge_slope[lo : lo + EDGE_CHUNK] = slope
        return silu.astype(BF16)

    hidden = edge_hidden([p0[...], p1[...], p2[...], p3[...]], th, pre_part, edge_w1, keep)
    hidden_sum = mm(st[...], hidden)
    node_slope, hidden_node, normed, inv_dev = node_body(h_ref[...], hidden_sum, node_w1, mix, node_w2)
    hidden_sum_o[...] = hidden_sum
    hidden_node_o[...] = hidden_node
    backward_body(
        cot[...], (edge_slope, node_slope, normed, inv_dev), gain[...], ss, ttst, w1t, back, n2t,
        (g0, g1, g2, g3), gpe_o, qr_o, gpn_o, gu_o, gain_o,
    )


def backward_kernel(
    own, p0, p1, p2, p3, spread, edge_slope, node_slope, normed, inv_dev, gain, ss, ttst, w1t, back, n2t,
    gpe_o, qr_o, gpn_o, gu_o, gain_o, up_o, *sends,
):
    up = landed(own, spread, p0, p1, p2, p3)
    up_o[...] = up
    backward_body(
        up, (edge_slope, node_slope[...], normed[...], inv_dev[:, :1]), gain[...], ss, ttst, w1t, back, n2t,
        sends, gpe_o, qr_o, gpn_o, gu_o, gain_o,
    )


def weight_args(refs):
    h_ref, p0, p1, p2, p3, feats, edge_w2, hidden_sum, hidden_node, back, gpe, qr, gpn, gu = refs
    gm = mm(gpn[...], back[:, L : 2 * L]).astype(BF16)
    h = h_ref[...]
    extended = jnp.concatenate([h, p0[...], p1[...], p2[...], p3[...]], axis=0)
    qr_high, qr_low = split(qr[...])
    h_high, h_low = split(hidden_sum[...])
    summed = (mm(h_high, edge_w2[...]) + mm(h_low, edge_w2[...])).astype(BF16)
    return (
        mm_t(extended, qr_high[: 2 * OWN]) + mm_t(extended, qr_low[: 2 * OWN]),
        mm_t(h, qr_high[2 * OWN :]) + mm_t(h, qr_low[2 * OWN :]),
        mm_t(feats[...], gpe[...]),
        mm_t(h_high, gm) + mm_t(h_low, gm),
        mm_t(h, gpn[...]),
        mm_t(summed, gpn[...]),
        mm_t(hidden_node[...], gu[...]),
    )


def weight_first_kernel(*refs):
    w1t, gain_in, acc, edge_acc, gain_acc = refs[14:]
    for i, term in enumerate(weight_args(refs[:14])):
        acc[i] = term
    edge_acc[...] = mm(refs[10][...], w1t[:, 2 * L :])
    gain_acc[...] = gain_in[...]


def weight_kernel(*refs):
    w1t, gain_in, acc_in, edge_in, gain_acc_in, acc, edge_acc, gain_acc = refs[14:]
    for i, term in enumerate(weight_args(refs[:14])):
        acc[i] = acc_in[i] + term
    edge_acc[...] = edge_in[...] + mm(refs[10][...], w1t[:, 2 * L :])
    gain_acc[...] = gain_acc_in[...] + gain_in[...]


def weight_last_kernel(*refs):
    gain_in, acc_in, gain_acc_in, out = refs[14:]
    core = lax.axis_index("c")
    terms = weight_args(refs[:14])
    for i, term in enumerate(terms):
        out[(i // 4) ^ core, (i % 4) * L : (i % 4 + 1) * L, :] = (acc_in[i] + term).astype(BF16)
    row = lax.broadcasted_iota(jnp.int32, (L, L), 0)
    gain = gain_acc_in[...] + gain_in[...]
    out[1 ^ core, 3 * L :, :] = jnp.where(row == 0, gain, 0.0).astype(BF16)


def edge_last_kernel(gpe, w1t, edge_in, out):
    out[...] = edge_in[...] + mm(gpe[...], w1t[:, 2 * L :])


def node_last_kernel(own, p0, p1, p2, p3, spread, out):
    out[...] = landed(own, spread, p0, p1, p2, p3)


def finish_kernel(factor, mine, half_ref, *refs):
    edge_in, edge_out, node_in, node_out, gain, buf, row, sems = refs[-8:]
    core = lax.axis_index("c")
    which = core if mine else 1 - core
    targets = (
        (edge_in.at[:L], edge_in.at[L : 2 * L], edge_in.at[2 * L :], edge_out),
        (node_in.at[:L], node_in.at[L :], node_out, gain),
    )

    def copies(half, i):
        source = row if half == 1 and i == 3 else buf.at[i * L : (i + 1) * L]
        return pltpu.make_async_copy(source, targets[half][i], sems.at[i])

    for i in range(4):
        block = half_ref[i * L : (i + 1) * L].astype(F32) * factor
        buf[i * L : (i + 1) * L] = block
        if i == 3:
            row[...] = block[0]
        for half in range(2):
            pl.when(which == half)(lambda half=half, i=i: copies(half, i).start())
    for half in range(2):
        for i in range(4):
            pl.when(which == half)(lambda half=half, i=i: copies(half, i).wait())


def finish(factor, mine, half, *parts):
    outs = [((3 * L, L), F32), ((L, L), F32), ((2 * L, L), F32), ((L, L), F32), ((L,), F32)]
    hbm = pl.BlockSpec(memory_space=pltpu.HBM)
    return pl.pallas_call(
        functools.partial(finish_kernel, factor, mine),
        out_shape=[jax.ShapeDtypeStruct(s, d) for s, d in outs],
        in_specs=[pl.BlockSpec(memory_space=pltpu.VMEM)] + [hbm] * len(parts),
        out_specs=[hbm] * 5,
        input_output_aliases={i + 1: i for i in range(len(parts))},
        scratch_shapes=[pltpu.VMEM((4 * L, L), F32), pltpu.VMEM((L,), F32), pltpu.SemaphoreType.DMA((4,))],
        compiler_params=pltpu.CompilerParams(vmem_limit_bytes=32 * 1024 * 1024),
    )(half, *parts)


def even_pairs(size):
    return [(i, i ^ 1) for i in range(size)]


def odd_pairs(size):
    up = [((i + 1) % size, (i + 2) % size) for i in range(0, size, 2)]
    return up + [(b, a) for a, b in up]


def exchange(parts):
    slabs = lax.axis_size(SLAB)
    regions = lax.axis_size(REGION)
    return [
        lax.ppermute(parts[0], REGION, odd_pairs(regions)),
        lax.ppermute(parts[1], REGION, even_pairs(regions)),
        lax.ppermute(parts[2], SLAB, odd_pairs(slabs)),
        lax.ppermute(parts[3], SLAB, even_pairs(slabs)),
    ]


def reduce_all(payload, late):
    keep = payload[0].astype(F32)
    got = lax.ppermute(payload[1], "c", [(0, 1), (1, 0)])
    part = (keep + got.astype(F32)).astype(BF16).reshape(CHUNKS, CHUNK_ROWS, L)
    part = lax.all_to_all(part, PLANE, 0, 0, tiled=True)
    part = jnp.sum(part.astype(F32), axis=0).astype(BF16)
    deep = lax.axis_size("z")
    part = lax.all_to_all(jnp.broadcast_to(part[None], (deep,) + part.shape), "z", 0, 0, tiled=True)
    part = jnp.sum(part.astype(F32), axis=0).astype(BF16)
    part, *late = lax.optimization_barrier((part, *late))
    part = jnp.broadcast_to(part[None], (CHUNKS,) + part.shape)
    mine = lax.all_to_all(part, PLANE, 0, 0, tiled=True).reshape(CHUNKS * CHUNK_ROWS, L)
    other = lax.ppermute(mine, "c", [(0, 1), (1, 0)])
    return mine, other, late


def local(
    nodes, feats, cotangent, edge_w1, edge_w2, node_w1, node_w2, ln_gain, senders, receivers, send_rows, edge_count
):
    edges = feats.shape[0]
    halo_outs = [((HALO, L), BF16)] * 4
    *sends, spread = call(
        first_kernel, halo_outs + [((OWN, 4 * HALO), BF16)], nodes, send_rows, space=pltpu.HBM,
        scratch_shapes=[pltpu.VMEM((OWN, L), BF16), pltpu.VMEM((4, HALO), jnp.int32), pltpu.SemaphoreType.DMA((2,))],
    )
    tos, th, ss, ttst, st, st_sent, pre_part, fw, w1t, back_w, n2t, mix, gain, edge_w1, feats, node_w1, edge_w2, node_w2, cotangent, nodes = call(
        prep_kernel,
        [
            ((edges, 4 * OWN), BF16), ((edges, 2 * OWN), BF16), ((edges, 2 * OWN), BF16), ((3 * OWN, edges), BF16),
            ((OWN, edges), BF16), ((OWN, edges), BF16), ((edges, L), F32),
            ((edges, L), F32), ((L, 3 * L), BF16), ((L, 4 * L), BF16), ((L, L), BF16), ((L, 2 * L), BF16),
            ((1, L), F32), ((3 * L, L), BF16), ((edges, L), BF16), ((2 * L, L), BF16), ((L, L), BF16), ((L, L), BF16),
            ((OWN, L), F32), ((OWN, L), BF16),
        ],
        edge_count, senders, receivers, ln_gain, edge_w1, feats, node_w1, edge_w2, node_w2, cotangent, nodes, spread,
        space=pltpu.HBM,
        free=(0, 11),
        scratch_shapes=[
            pltpu.VMEM((OWN, 4 * HALO), BF16), pltpu.SMEM((1, 1), jnp.int32),
            pltpu.VMEM((edges,), jnp.int32), pltpu.VMEM((edges,), jnp.int32),
            pltpu.VMEM((L,), F32), pltpu.SemaphoreType.DMA((12,)),
        ],
    )
    h = nodes
    saved = []
    for _ in range(STEPS - 1):
        halo = exchange(sends)
        *sends, pre, hidden = call(
            forward_kernel,
            halo_outs + [((edges, L), F32), ((edges, L), BF16)],
            *halo, *sends, pre_part, th, st_sent, edge_w1, node_w1, mix, node_w2, gain,
        )
        nxt, pre_part, *rest = call(
            own_kernel,
            [
                ((OWN, L), BF16), ((edges, L), F32), ((edges, L), F32), ((OWN, L), F32), ((OWN, L), F32), ((OWN, L), BF16),
                ((OWN, L), F32), ((OWN, 128), F32),
            ],
            h, pre, hidden, st, tos, fw, edge_w1, node_w1, mix, node_w2, gain,
        )
        saved.append((h, halo, rest))
        h = nxt
    halo = exchange(sends)
    back_outs = [
        ((edges, L), BF16), ((3 * OWN, L), F32), ((OWN, L), BF16), ((OWN, L), BF16), ((1, L), F32),
    ]
    g0, g1, g2, g3, *terms, gain_term, hidden_sum, hidden_node = call(
        turn_kernel,
        halo_outs + back_outs + [((OWN, L), F32), ((OWN, L), BF16)],
        h, *halo, pre_part, th, st, edge_w1, node_w1, mix, node_w2, gain, cotangent, ss, ttst, w1t, back_w, n2t,
        scratch_shapes=[pltpu.VMEM((edges, L), F32)],
    )
    back = exchange([g0, g1, g2, g3])
    own_out = [((OWN, L), F32)]
    (own,) = call(rest_kernel, own_out, cotangent, terms[1], terms[2], w1t, back_w)
    acc_outs = [((7, L, L), F32), ((edges, L), F32), ((1, L), F32)]
    totals = call(
        weight_first_kernel, acc_outs, h, *halo, feats, edge_w2, hidden_sum, hidden_node, back_w, *terms, w1t, gain_term
    )
    for layer in reversed(range(STEPS - 1)):
        h, halo, (edge_slope, hidden_sum, node_slope, hidden_node, normed, inv_dev) = saved[layer]
        back, totals = lax.optimization_barrier((back, totals))
        gpe, qr, gpn, gu, gain_term, up, *sends = call(
            backward_kernel, back_outs + own_out + (halo_outs if layer > 0 else []),
            own, *back, spread, edge_slope, node_slope, normed, inv_dev, gain, ss, ttst, w1t, back_w, n2t,
        )
        terms = (gpe, qr, gpn, gu)
        rest_outs = own_out if layer > 0 else own_out + halo_outs
        own, *late = call(rest_kernel, rest_outs, up, terms[1], terms[2], w1t, back_w)
        back = exchange(sends + late)
        shared = (h, *halo, feats, edge_w2, hidden_sum, hidden_node, back_w, *terms)
        if layer > 0:
            totals = call(weight_kernel, acc_outs, *shared, w1t, gain_term, *totals)
    (payload,) = call(
        weight_last_kernel, [((2, 4 * L, L), BF16)], *shared, gain_term, totals[0], totals[2]
    )
    (edge_grad,) = call(edge_last_kernel, [((edges, L), F32)], terms[0], w1t, totals[1])
    (node_grad,) = call(node_last_kernel, [((OWN, L), F32)], own, *back, spread)
    mine, other, (node_grad, edge_grad) = reduce_all(payload, (node_grad, edge_grad))
    devices = lax.axis_size(REGION) * lax.axis_size(SLAB)
    factor = float(OWN * devices) ** (-0.5)

    parts = finish(factor, True, mine)
    edge_in, edge_out, node_in, node_out, gain_grad = finish(factor, False, other, *parts)
    return node_grad, edge_grad, edge_in, edge_out, node_in, node_out, gain_grad


def solution(mesh):
    fine = Mesh(mesh.devices.reshape(4, 2, 8, 2, 2), AXES)
    split_rows = P(AXES, None)
    placed = (
        split_rows, split_rows, split_rows, P(), P(), P(), P(), P(), P(AXES), P(AXES), split_rows, P(REGION, SLAB),
    )
    return jax.shard_map(
        local,
        mesh=fine,
        in_specs=placed,
        out_specs=(split_rows, split_rows, P(), P(), P(), P(), P()),
        check_vma=False,
    )
```

```python
import functools

import jax
import jax.numpy as jnp
from jax import lax
from jax.experimental import pallas as pl
from jax.experimental.pallas import tpu as pltpu
from jax.sharding import Mesh
from jax.sharding import PartitionSpec as P

STEPS = 4
EPS = 1e-05
L = 256
OWN = 128
HALO = 32
BF16 = jnp.bfloat16
F32 = jnp.float32
AXES = ("x", "yh", "z", "yl", "c")
REGION = ("x", "yh")
SLAB = ("z", "yl", "c")
PLANE = ("yl", "yh", "x")
CHUNK = 128
EDGE_CHUNK = 640
CHUNKS = 16
CHUNK_ROWS = 64


def mm(a, b):
    return jnp.dot(a, b, preferred_element_type=F32)


def mm_t(a, b):
    return lax.dot_general(a, b, (((0,), (0,)), ((), ())), preferred_element_type=F32)


def split(v):
    high = v.astype(BF16)
    low = (v - high.astype(F32)).astype(BF16)
    return high, low


def mm_split(v, w):
    high, low = split(v)
    return mm(high, w) + mm(low, w)


def sigmoid(v):
    return 0.5 * jnp.tanh(0.5 * v) + 0.5


def call(kernel, outs, *args, space=pltpu.VMEM, free=(), **kw):
    specs = [pl.BlockSpec(memory_space=pl.ANY if i in free else space) for i in range(len(args))]
    if space is pltpu.HBM:
        args = [a if i in free else pltpu.with_memory_space_constraint(a, space) for i, a in enumerate(args)]
    return pl.pallas_call(
        kernel,
        out_shape=[jax.ShapeDtypeStruct(s, d) for s, d in outs],
        in_specs=specs,
        out_specs=[pl.BlockSpec(memory_space=pltpu.VMEM)] * len(outs),
        compiler_params=pltpu.CompilerParams(vmem_limit_bytes=32 * 1024 * 1024),
        **kw,
    )(*args)


def slot_lists(lists):
    slab_odd = lax.axis_index("c")
    region_odd = lax.axis_index("yh")
    a, b, c, d = (lists[i : i + 1, :] for i in range(4))
    return (
        jnp.where(region_odd == 1, d, c),
        jnp.where(region_odd == 1, c, d),
        jnp.where(slab_odd == 1, b, a),
        jnp.where(slab_odd == 1, a, b),
    )


def first_kernel(nodes, lists, s0, s1, s2, s3, spread, h, rows, sems):
    copies = [pltpu.make_async_copy(nodes, h, sems.at[0]), pltpu.make_async_copy(lists, rows, sems.at[1])]
    for copy in copies:
        copy.start()
    copies[1].wait()
    row = lax.broadcasted_iota(jnp.int32, (OWN, HALO), 0)
    hots = [(row == idx).astype(F32).astype(BF16) for idx in slot_lists(rows[...])]
    copies[0].wait()
    for i, (hot, out) in enumerate(zip(hots, (s0, s1, s2, s3))):
        spread[:, i * HALO : (i + 1) * HALO] = hot
        out[...] = mm_t(hot, h[...]).astype(BF16)


def prep_kernel(
    count_in, send_in, recv_in, gain_in, w1_in, feats_in, n1_in, w2_in, n2_in, cot_in, nodes_in, spread_in,
    tos_out, th_out, ss_out, ttst_out, st_out, st_sent_out, pre_out, fw_out, w1t_out, back_out, n2t_out, mix_out,
    gain_out, w1, feats, n1, w2, n2, cot, nodes,
    spread, count, send_idx, recv_idx, gain, sems,
):
    pairs = (
        (w1_in, w1), (feats_in, feats), (count_in, count), (spread_in, spread), (send_in, send_idx), (recv_in, recv_idx),
        (n1_in, n1), (w2_in, w2), (n2_in, n2), (nodes_in, nodes), (gain_in, gain), (cot_in, cot),
    )
    copies = [pltpu.make_async_copy(a, b, sems.at[i]) for i, (a, b) in enumerate(pairs)]
    for copy in copies:
        copy.start()
    for copy in copies:
        copy.wait()
    edges = feats.shape[0]
    lane = lax.broadcasted_iota(jnp.int32, (1, edges), 1)
    live = lane < count[0, 0]
    snd = send_idx[...].reshape(1, edges)
    off = snd - OWN
    slab_swap = jnp.where(lax.axis_index("c") == 1, 3 * HALO, 2 * HALO)
    region_swap = jnp.where(lax.axis_index("yh") == 1, 3 * HALO, 2 * HALO)
    flip = jnp.where(off < 2 * HALO, slab_swap, region_swap)
    snd = jnp.where(off >= 0, OWN + (off ^ flip), snd)
    snd = jnp.where(live, snd, -1)
    rcv = jnp.where(live, recv_idx[...].reshape(1, edges), -1)
    tt = (lax.broadcasted_iota(jnp.int32, (2 * OWN, edges), 0) == snd).astype(F32)
    st = (lax.broadcasted_iota(jnp.int32, (OWN, edges), 0) == rcv).astype(F32)
    spread_t = spread[...].T
    tt16 = tt.astype(BF16)
    st16 = st.astype(BF16)
    t16 = tt.T.astype(BF16)
    s16 = st.T.astype(BF16)
    ttst_out[: 2 * OWN] = tt16
    ttst_out[2 * OWN :] = st16
    st_out[...] = st16
    st_sent_out[...] = mm(spread_t, st16).astype(BF16)
    for i in range(2):
        tos_out[:, i * OWN : (i + 1) * OWN] = t16[:, :OWN]
        th_out[:, i * OWN : (i + 1) * OWN] = t16[:, OWN:]
        tos_out[:, (2 + i) * OWN : (3 + i) * OWN] = s16
        ss_out[:, i * OWN : (i + 1) * OWN] = s16
    fw_out[...] = mm(feats[...], w1[2 * L :])
    own_pre(nodes[...], tos_out, fw_out, w1, pre_out)
    w1t_out[...] = w1[...].T
    n2t_out[...] = n2[...].T
    mix_high, mix_low = split(mm(w2[...], n1[L:]))
    mix_out[:, :L] = mix_high
    mix_out[:, L:] = mix_low
    back_out[:, : 2 * L] = n1[...].T
    back_out[:, 2 * L : 3 * L] = mix_high.T
    back_out[:, 3 * L :] = mix_low.T
    gain_out[...] = gain[...].reshape(1, L)


def edge_hidden(halo, th, pre_part, edge_w1, keep):
    high, low = split(mm(jnp.concatenate(halo, axis=0), edge_w1[:L]))
    table = jnp.concatenate([high, low], axis=0)
    hidden = []
    for lo in range(0, pre_part.shape[0], EDGE_CHUNK):
        pre = mm(th[lo : lo + EDGE_CHUNK], table) + pre_part[lo : lo + EDGE_CHUNK]
        hidden.append(keep(lo, pre))
    return jnp.concatenate(hidden, axis=0)


def edge_slopes(pre):
    sig = sigmoid(pre)
    silu = pre * sig
    return silu, sig + silu * (1.0 - sig)


def node_body(h, hidden_sum, node_w1, mix, node_w2):
    high, low = split(hidden_sum)
    pre_node = mm(h, node_w1[:L]) + mm(high, mix[:, :L]) + mm(high, mix[:, L:]) + mm(low, mix[:, :L])
    silu_n, node_slope = edge_slopes(pre_node)
    hidden_node = silu_n.astype(BF16)
    update = mm(hidden_node, node_w2[...])
    centre = update - jnp.mean(update, axis=-1, keepdims=True)
    inv_dev = lax.rsqrt(jnp.mean(centre * centre, axis=-1, keepdims=True) + EPS)
    return node_slope, hidden_node, centre * inv_dev, inv_dev


def own_pre(h, tos, fw, edge_w1, out):
    far_high, far_low = split(mm(h, edge_w1[:L]))
    near_high, near_low = split(mm(h, edge_w1[L : 2 * L]))
    table = jnp.concatenate([far_high, far_low, near_high, near_low], axis=0)
    for lo in range(0, fw.shape[0], CHUNK):
        out[lo : lo + CHUNK] = mm(tos[lo : lo + CHUNK], table) + fw[lo : lo + CHUNK]


def forward_kernel(
    p0, p1, p2, p3, q0, q1, q2, q3, pre_part, th, st_sent, edge_w1, node_w1, mix, node_w2, gain,
    s0, s1, s2, s3, pre_o, hidden_o,
):
    def keep(lo, pre):
        pre_o[lo : lo + EDGE_CHUNK] = pre
        part = (pre * sigmoid(pre)).astype(BF16)
        hidden_o[lo : lo + EDGE_CHUNK] = part
        return part

    hidden = edge_hidden([p0[...], p1[...], p2[...], p3[...]], th, pre_part, edge_w1, keep)
    h = jnp.concatenate([q0[...], q1[...], q2[...], q3[...]], axis=0)
    normed = node_body(h, mm(st_sent[...], hidden), node_w1, mix, node_w2)[2]
    sent = (h.astype(F32) + normed * gain[...]).astype(BF16)
    for i, out in enumerate((s0, s1, s2, s3)):
        out[...] = sent[i * HALO : (i + 1) * HALO]


def own_kernel(
    h_ref, pre, hidden, st, tos, fw, edge_w1, node_w1, mix, node_w2, gain,
    h_out, pre_part_o, edge_slope_o, hidden_sum_o, node_slope_o, hidden_node_o, normed_o, inv_dev_o,
):
    h = h_ref[...]
    hidden_sum = mm(st[...], hidden[...])
    node_slope, hidden_node, normed, inv_dev = node_body(h, hidden_sum, node_w1, mix, node_w2)
    nxt = (h.astype(F32) + normed * gain[...]).astype(BF16)
    h_out[...] = nxt
    own_pre(nxt, tos, fw, edge_w1, pre_part_o)
    edge_slope_o[...] = edge_slopes(pre[...])[1]
    hidden_sum_o[...] = hidden_sum
    node_slope_o[...] = node_slope
    hidden_node_o[...] = hidden_node
    normed_o[...] = normed
    inv_dev_o[...] = jnp.broadcast_to(inv_dev, inv_dev_o.shape)


def backward_body(
    up, parts, gain, ss, ttst, w1t, back, n2t, sends, gpe_o, qr_o, gpn_o, gu_o, gain_o
):
    edge_slope, node_slope, normed, inv_dev = parts
    gain_o[...] = jnp.sum(up * normed, axis=0, keepdims=True)
    scaled = up * gain
    gu = inv_dev * (
        scaled
        - jnp.mean(scaled, axis=-1, keepdims=True)
        - normed * jnp.mean(scaled * normed, axis=-1, keepdims=True)
    )
    gu = gu.astype(BF16)
    gpn = (mm(gu, n2t[...]) * node_slope).astype(BF16)
    gu_o[...] = gu
    gpn_o[...] = gpn
    gh = mm(gpn, back[:, 2 * L : 3 * L]) + mm(gpn, back[:, 3 * L :])
    gh = gh.astype(BF16)
    gpe = []
    for lo in range(0, edge_slope.shape[0], CHUNK):
        part = (mm(ss[lo : lo + CHUNK, :OWN], gh) * edge_slope[lo : lo + CHUNK]).astype(BF16)
        gpe_o[lo : lo + CHUNK] = part
        gpe.append(part)
    qr = mm(ttst[...], jnp.concatenate(gpe, axis=0))
    if sends:
        halo_grads(qr, w1t, sends)
    qr_o[...] = qr


def halo_grads(qr, w1t, sends):
    ge = mm(qr[OWN : 2 * OWN].astype(BF16), w1t[:, :L])
    for i, out in enumerate(sends):
        out[...] = ge[i * HALO : (i + 1) * HALO].astype(BF16)


def rest_kernel(up, qr, gpn, w1t, back, own_out, *sends):
    if sends:
        halo_grads(qr, w1t, sends)
    q_high, q_low = split(qr[:OWN])
    r_high, r_low = split(qr[2 * OWN :])
    far, near = w1t[:, :L], w1t[:, L : 2 * L]
    own_out[...] = (
        up[...] + mm(gpn[...], back[:, :L]) + mm(q_high, far) + mm(q_low, far) + mm(r_high, near) + mm(r_low, near)
    )


def landed(own, spread, p0, p1, p2, p3):
    parts = jnp.concatenate([p0[...], p1[...], p2[...], p3[...]], axis=0)
    return own[...] + mm(spread[...], parts)


def turn_kernel(
    h_ref, p0, p1, p2, p3, pre_part, th, st, edge_w1, node_w1, mix, node_w2, gain, cot, ss, ttst, w1t, back, n2t,
    g0, g1, g2, g3, gpe_o, qr_o, gpn_o, gu_o, gain_o, hidden_sum_o, hidden_node_o, edge_slope,
):
    def keep(lo, pre):
        silu, slope = edge_slopes(pre)
        edge_slope[lo : lo + EDGE_CHUNK] = slope
        return silu.astype(BF16)

    hidden = edge_hidden([p0[...], p1[...], p2[...], p3[...]], th, pre_part, edge_w1, keep)
    hidden_sum = mm(st[...], hidden)
    node_slope, hidden_node, normed, inv_dev = node_body(h_ref[...], hidden_sum, node_w1, mix, node_w2)
    hidden_sum_o[...] = hidden_sum
    hidden_node_o[...] = hidden_node
    backward_body(
        cot[...], (edge_slope, node_slope, normed, inv_dev), gain[...], ss, ttst, w1t, back, n2t,
        (g0, g1, g2, g3), gpe_o, qr_o, gpn_o, gu_o, gain_o,
    )


def backward_kernel(
    own, p0, p1, p2, p3, spread, edge_slope, node_slope, normed, inv_dev, gain, ss, ttst, w1t, back, n2t,
    gpe_o, qr_o, gpn_o, gu_o, gain_o, up_o, *sends,
):
    up = landed(own, spread, p0, p1, p2, p3)
    up_o[...] = up
    backward_body(
        up, (edge_slope, node_slope[...], normed[...], inv_dev[:, :1]), gain[...], ss, ttst, w1t, back, n2t,
        sends, gpe_o, qr_o, gpn_o, gu_o, gain_o,
    )


def weight_args(refs):
    h_ref, p0, p1, p2, p3, feats, edge_w2, hidden_sum, hidden_node, back, gpe, qr, gpn, gu = refs
    gm = mm(gpn[...], back[:, L : 2 * L]).astype(BF16)
    h = h_ref[...]
    extended = jnp.concatenate([h, p0[...], p1[...], p2[...], p3[...]], axis=0)
    qr_high, qr_low = split(qr[...])
    h_high, h_low = split(hidden_sum[...])
    summed = (mm(h_high, edge_w2[...]) + mm(h_low, edge_w2[...])).astype(BF16)
    return (
        mm_t(extended, qr_high[: 2 * OWN]) + mm_t(extended, qr_low[: 2 * OWN]),
        mm_t(h, qr_high[2 * OWN :]) + mm_t(h, qr_low[2 * OWN :]),
        mm_t(feats[...], gpe[...]),
        mm_t(h_high, gm) + mm_t(h_low, gm),
        mm_t(h, gpn[...]),
        mm_t(summed, gpn[...]),
        mm_t(hidden_node[...], gu[...]),
    )


def weight_first_kernel(*refs):
    w1t, gain_in, acc, edge_acc, gain_acc = refs[14:]
    for i, term in enumerate(weight_args(refs[:14])):
        acc[i] = term
    edge_acc[...] = mm(refs[10][...], w1t[:, 2 * L :])
    gain_acc[...] = gain_in[...]


def weight_kernel(*refs):
    w1t, gain_in, acc_in, edge_in, gain_acc_in, acc, edge_acc, gain_acc = refs[14:]
    for i, term in enumerate(weight_args(refs[:14])):
        acc[i] = acc_in[i] + term
    edge_acc[...] = edge_in[...] + mm(refs[10][...], w1t[:, 2 * L :])
    gain_acc[...] = gain_acc_in[...] + gain_in[...]


def weight_last_kernel(*refs):
    gain_in, acc_in, gain_acc_in, out = refs[14:]
    core = lax.axis_index("c")
    terms = weight_args(refs[:14])
    for i, term in enumerate(terms):
        out[(i // 4) ^ core, (i % 4) * L : (i % 4 + 1) * L, :] = (acc_in[i] + term).astype(BF16)
    row = lax.broadcasted_iota(jnp.int32, (L, L), 0)
    gain = gain_acc_in[...] + gain_in[...]
    out[1 ^ core, 3 * L :, :] = jnp.where(row == 0, gain, 0.0).astype(BF16)


def edge_last_kernel(gpe, w1t, edge_in, out):
    out[...] = edge_in[...] + mm(gpe[...], w1t[:, 2 * L :])


def node_last_kernel(own, p0, p1, p2, p3, spread, out):
    out[...] = landed(own, spread, p0, p1, p2, p3)


def finish_kernel(factor, mine, half_ref, *refs):
    edge_in, edge_out, node_in, node_out, gain, buf, row, sems = refs[-8:]
    core = lax.axis_index("c")
    which = core if mine else 1 - core
    targets = (
        (edge_in.at[:L], edge_in.at[L : 2 * L], edge_in.at[2 * L :], edge_out),
        (node_in.at[:L], node_in.at[L :], node_out, gain),
    )

    def copies(half, i):
        source = row if half == 1 and i == 3 else buf.at[i * L : (i + 1) * L]
        return pltpu.make_async_copy(source, targets[half][i], sems.at[i])

    for i in range(4):
        block = half_ref[i * L : (i + 1) * L].astype(F32) * factor
        buf[i * L : (i + 1) * L] = block
        if i == 3:
            row[...] = block[0]
        for half in range(2):
            pl.when(which == half)(lambda half=half, i=i: copies(half, i).start())
    for half in range(2):
        for i in range(4):
            pl.when(which == half)(lambda half=half, i=i: copies(half, i).wait())


def finish(factor, mine, half, *parts):
    outs = [((3 * L, L), F32), ((L, L), F32), ((2 * L, L), F32), ((L, L), F32), ((L,), F32)]
    hbm = pl.BlockSpec(memory_space=pltpu.HBM)
    return pl.pallas_call(
        functools.partial(finish_kernel, factor, mine),
        out_shape=[jax.ShapeDtypeStruct(s, d) for s, d in outs],
        in_specs=[pl.BlockSpec(memory_space=pltpu.VMEM)] + [hbm] * len(parts),
        out_specs=[hbm] * 5,
        input_output_aliases={i + 1: i for i in range(len(parts))},
        scratch_shapes=[pltpu.VMEM((4 * L, L), F32), pltpu.VMEM((L,), F32), pltpu.SemaphoreType.DMA((4,))],
        compiler_params=pltpu.CompilerParams(vmem_limit_bytes=32 * 1024 * 1024),
    )(half, *parts)


def even_pairs(size):
    return [(i, i ^ 1) for i in range(size)]


def odd_pairs(size):
    up = [((i + 1) % size, (i + 2) % size) for i in range(0, size, 2)]
    return up + [(b, a) for a, b in up]


def exchange(parts):
    slabs = lax.axis_size(SLAB)
    regions = lax.axis_size(REGION)
    return [
        lax.ppermute(parts[0], REGION, odd_pairs(regions)),
        lax.ppermute(parts[1], REGION, even_pairs(regions)),
        lax.ppermute(parts[2], SLAB, odd_pairs(slabs)),
        lax.ppermute(parts[3], SLAB, even_pairs(slabs)),
    ]


def reduce_all(payload, late):
    keep = payload[0].astype(F32)
    got = lax.ppermute(payload[1], "c", [(0, 1), (1, 0)])
    part = (keep + got.astype(F32)).astype(BF16).reshape(CHUNKS, CHUNK_ROWS, L)
    part = lax.all_to_all(part, PLANE, 0, 0, tiled=True)
    part = jnp.sum(part.astype(F32), axis=0).astype(BF16)
    deep = lax.axis_size("z")
    part = lax.all_to_all(jnp.broadcast_to(part[None], (deep,) + part.shape), "z", 0, 0, tiled=True)
    part = jnp.sum(part.astype(F32), axis=0).astype(BF16)
    part, *late = lax.optimization_barrier((part, *late))
    part = jnp.broadcast_to(part[None], (CHUNKS,) + part.shape)
    mine = lax.all_to_all(part, PLANE, 0, 0, tiled=True).reshape(CHUNKS * CHUNK_ROWS, L)
    other = lax.ppermute(mine, "c", [(0, 1), (1, 0)])
    return mine, other, late


def local(
    nodes, feats, cotangent, edge_w1, edge_w2, node_w1, node_w2, ln_gain, senders, receivers, send_rows, edge_count
):
    edges = feats.shape[0]
    halo_outs = [((HALO, L), BF16)] * 4
    *sends, spread = call(
        first_kernel, halo_outs + [((OWN, 4 * HALO), BF16)], nodes, send_rows, space=pltpu.HBM,
        scratch_shapes=[pltpu.VMEM((OWN, L), BF16), pltpu.VMEM((4, HALO), jnp.int32), pltpu.SemaphoreType.DMA((2,))],
    )
    tos, th, ss, ttst, st, st_sent, pre_part, fw, w1t, back_w, n2t, mix, gain, edge_w1, feats, node_w1, edge_w2, node_w2, cotangent, nodes = call(
        prep_kernel,
        [
            ((edges, 4 * OWN), BF16), ((edges, 2 * OWN), BF16), ((edges, 2 * OWN), BF16), ((3 * OWN, edges), BF16),
            ((OWN, edges), BF16), ((OWN, edges), BF16), ((edges, L), F32),
            ((edges, L), F32), ((L, 3 * L), BF16), ((L, 4 * L), BF16), ((L, L), BF16), ((L, 2 * L), BF16),
            ((1, L), F32), ((3 * L, L), BF16), ((edges, L), BF16), ((2 * L, L), BF16), ((L, L), BF16), ((L, L), BF16),
            ((OWN, L), F32), ((OWN, L), BF16),
        ],
        edge_count, senders, receivers, ln_gain, edge_w1, feats, node_w1, edge_w2, node_w2, cotangent, nodes, spread,
        space=pltpu.HBM,
        free=(0, 11),
        scratch_shapes=[
            pltpu.VMEM((OWN, 4 * HALO), BF16), pltpu.SMEM((1, 1), jnp.int32),
            pltpu.VMEM((edges,), jnp.int32), pltpu.VMEM((edges,), jnp.int32),
            pltpu.VMEM((L,), F32), pltpu.SemaphoreType.DMA((12,)),
        ],
    )
    h = nodes
    saved = []
    for _ in range(STEPS - 1):
        halo = exchange(sends)
        *sends, pre, hidden = call(
            forward_kernel,
            halo_outs + [((edges, L), F32), ((edges, L), BF16)],
            *halo, *sends, pre_part, th, st_sent, edge_w1, node_w1, mix, node_w2, gain,
        )
        nxt, pre_part, *rest = call(
            own_kernel,
            [
                ((OWN, L), BF16), ((edges, L), F32), ((edges, L), F32), ((OWN, L), F32), ((OWN, L), F32), ((OWN, L), BF16),
                ((OWN, L), F32), ((OWN, 128), F32),
            ],
            h, pre, hidden, st, tos, fw, edge_w1, node_w1, mix, node_w2, gain,
        )
        saved.append((h, halo, rest))
        h = nxt
    halo = exchange(sends)
    back_outs = [
        ((edges, L), BF16), ((3 * OWN, L), F32), ((OWN, L), BF16), ((OWN, L), BF16), ((1, L), F32),
    ]
    g0, g1, g2, g3, *terms, gain_term, hidden_sum, hidden_node = call(
        turn_kernel,
        halo_outs + back_outs + [((OWN, L), F32), ((OWN, L), BF16)],
        h, *halo, pre_part, th, st, edge_w1, node_w1, mix, node_w2, gain, cotangent, ss, ttst, w1t, back_w, n2t,
        scratch_shapes=[pltpu.VMEM((edges, L), F32)],
    )
    back = exchange([g0, g1, g2, g3])
    own_out = [((OWN, L), F32)]
    (own,) = call(rest_kernel, own_out, cotangent, terms[1], terms[2], w1t, back_w)
    acc_outs = [((7, L, L), F32), ((edges, L), F32), ((1, L), F32)]
    totals = call(
        weight_first_kernel, acc_outs, h, *halo, feats, edge_w2, hidden_sum, hidden_node, back_w, *terms, w1t, gain_term
    )
    for layer in reversed(range(STEPS - 1)):
        h, halo, (edge_slope, hidden_sum, node_slope, hidden_node, normed, inv_dev) = saved[layer]
        back, totals = lax.optimization_barrier((back, totals))
        gpe, qr, gpn, gu, gain_term, up, *sends = call(
            backward_kernel, back_outs + own_out + (halo_outs if layer > 0 else []),
            own, *back, spread, edge_slope, node_slope, normed, inv_dev, gain, ss, ttst, w1t, back_w, n2t,
        )
        terms = (gpe, qr, gpn, gu)
        rest_outs = own_out if layer > 0 else own_out + halo_outs
        own, *late = call(rest_kernel, rest_outs, up, terms[1], terms[2], w1t, back_w)
        back = exchange(sends + late)
        shared = (h, *halo, feats, edge_w2, hidden_sum, hidden_node, back_w, *terms)
        if layer > 0:
            totals = call(weight_kernel, acc_outs, *shared, w1t, gain_term, *totals)
    (payload,) = call(
        weight_last_kernel, [((2, 4 * L, L), BF16)], *shared, gain_term, totals[0], totals[2]
    )
    (edge_grad,) = call(edge_last_kernel, [((edges, L), F32)], terms[0], w1t, totals[1])
    (node_grad,) = call(node_last_kernel, [((OWN, L), F32)], own, *back, spread)
    mine, other, (node_grad, edge_grad) = reduce_all(payload, (node_grad, edge_grad))
    devices = lax.axis_size(REGION) * lax.axis_size(SLAB)
    factor = float(OWN * devices) ** (-0.5)

    parts = finish(factor, True, mine)
    edge_in, edge_out, node_in, node_out, gain_grad = finish(factor, False, other, *parts)
    return node_grad, edge_grad, edge_in, edge_out, node_in, node_out, gain_grad


def solution(mesh):
    fine = Mesh(mesh.devices.reshape(4, 2, 8, 2, 2), AXES)
    split_rows = P(AXES, None)
    placed = (
        split_rows, split_rows, split_rows, P(), P(), P(), P(), P(), P(AXES), P(AXES), split_rows, P(REGION, SLAB),
    )
    return jax.shard_map(
        local,
        mesh=fine,
        in_specs=placed,
        out_specs=(split_rows, split_rows, P(), P(), P(), P(), P()),
        check_vma=False,
    )
```
